32 devices in a mesh: pos: 4 (over x, core), seq: 8 (over z, y).
Axes of the slice: x: 2, y: 2, z: 4, core: 2. Of those that a mesh axis runs over, the one named last changes fastest.
Arguments:
- tokens: bfloat16 [1024, 32, 768], P('pos', 'seq'), may hold values from -6 to 6
- cotangent: bfloat16 [1024, 32, 768], P('pos', 'seq'), may hold values from -6 to 6
- gains: float32 [2, 768], replicated, may hold values from 0.5 to 1.5
- gain_first: float32 [2, 768], replicated, may hold values from -54.3058 to 54.3058
- gain_second: float32 [2, 768], replicated, may hold values from 11.239424 to 80.2816
- mix_logits: float32 [12, 1024, 1024], P(None, None, 'pos'), may hold values from -9 to 9
- logit_first: float32 [12, 1024, 1024], P(None, None, 'pos'), may hold values from -95.57821 to 95.57821, as said below
- logit_second: float32 [12, 1024, 1024], P(None, None, 'pos'), may hold values from 2e-10 to 236.97818, as said below
- w_value: float32 [768, 768], P('seq'), may hold values from -0.21875 to 0.21875
- value_first: float32 [768, 768], P('seq'), may hold values from -63.356766 to 63.356766
- value_second: float32 [768, 768], P('seq'), may hold values from 14.680064 to 104.8576
- w_out: float32 [768, 768], P('seq'), may hold values from -1.75 to 1.75
- out_first: float32 [768, 768], P('seq'), may hold values from -12.44508 to 12.44508
- out_second: float32 [768, 768], P('seq'), may hold values from 0.56 to 4
- w_up: float32 [768, 3072], P('seq'), may hold values from -0.21875 to 0.21875
- up_first: float32 [768, 3072], P('seq'), may hold values from -23.532515 to 23.532515
- up_second: float32 [768, 3072], P('seq'), may hold values from 2.064384 to 14.7456
- w_down: float32 [3072, 768], P('seq'), may hold values from -0.109375 to 0.109375
- down_first: float32 [3072, 768], P('seq'), may hold values from -47.06503 to 47.06503
- down_second: float32 [3072, 768], P('seq'), may hold values from 8.257536 to 58.9824
Outputs:
- output: bfloat16 [1024, 32, 768], P('pos', 'seq')
- input_grad: bfloat16 [1024, 32, 768], P('pos', 'seq')
- gains_new: float32 [2, 768], replicated
- gain_first_new: float32 [2, 768], replicated
- gain_second_new: float32 [2, 768], replicated
- logits_new: float32 [12, 1024, 1024], P(None, None, 'pos')
- logit_first_new: float32 [12, 1024, 1024], P(None, None, 'pos')
- logit_second_new: float32 [12, 1024, 1024], P(None, None, 'pos')
- value_new: float32 [768, 768], P('seq')
- value_first_new: float32 [768, 768], P('seq')
- value_second_new: float32 [768, 768], P('seq')
- out_new: float32 [768, 768], P('seq')
- out_first_new: float32 [768, 768], P('seq')
- out_second_new: float32 [768, 768], P('seq')
- up_new: float32 [768, 3072], P('seq')
- up_first_new: float32 [768, 3072], P('seq')
- up_second_new: float32 [768, 3072], P('seq')
- down_new: float32 [3072, 768], P('seq')
- down_first_new: float32 [3072, 768], P('seq')
- down_second_new: float32 [3072, 768], P('seq')
The draws below stay inside these ranges and needn't reach their ends.
Inputs may be any that keep to these rules, and one draw needn't show every extreme that they name: `logit_first`: first moments of both signs. `logit_second`: positive.
All inputs are finite; a program needn't handle non-finite values.
Results may differ from the reference program's by a relative error of at most 0.0085.
Values may be sent and summed in bfloat16 or wider, within the bound.
No kernel may reach another device: no remote copies, remote signals or barrier semaphores. Data moves between devices by JAX's collectives and lax.ppermute only.
A program may use at most 256 MiB of HBM per device.

```python
import math
import jax
import jax.numpy as jnp
from jax import lax

D = 768
H = 12
HD = 64
FF = 3072
L = 1024
STEP = 10
SEQS = 32
TOKENS = 32768


def row_scale():
    rows = jnp.arange(L, dtype=jnp.float32)
    first_row = jnp.where(rows < 0.5, 0.05, 1.0)
    return 0.3 * jnp.sqrt(jnp.float32(TOKENS * HD)) * first_row / (rows + 1.0)


def column_factor():
    rows = jnp.arange(L, dtype=jnp.int32)
    return jnp.where(rows[None, :] <= rows[:, None], 1.0, 0.05).astype(jnp.float32)


def draw_logit_first(key, part):
    key = jax.random.fold_in(key, 11)
    normal_draw = jax.random.truncated_normal(key, -4.0, 4.0, (H, L, L), jnp.float32)
    return 0.11 * normal_draw * (row_scale()[:, None] * column_factor())[None]


def draw_logit_second(key, part):
    key = jax.random.fold_in(key, 23)
    spread = jax.random.uniform(key, (H, L, L), jnp.float32, math.log(0.7), math.log(5.0))
    scaled = row_scale()[:, None] * column_factor()
    return 0.001 * jnp.exp(spread) * (scaled * scaled)[None]


def block_scale(stream_key, dims, split, smallest, high):
    def one(position, shards_of):
        draws = jax.random.uniform(jax.random.fold_in(jax.random.fold_in(stream_key, 6), position), (shards_of,), jnp.float32, smallest / len(split), high / len(split))
        return jnp.repeat(jnp.exp(draws), dims[position] // shards_of).reshape((-1,) + (1,) * (len(dims) - position - 1))

    level = one(*split[0])
    for cut in split[1:]:
        level = level * one(*cut)
    return level


def scatter_about(stream_key, extent, scale, bound, shards=(), held_as=jnp.bfloat16):
    level = block_scale(stream_key, extent, shards, -0.22, 0.18) if shards else 1.0
    entries = jax.random.normal(stream_key, extent, jnp.float32) * scale * level
    return jnp.minimum(jnp.maximum(entries, -bound), bound).astype(held_as)


def setup_inputs(seed: int = 0) -> dict:
    seeds = jax.random.split(jax.random.key(seed), 21)
    tokens = scatter_about(seeds[0], (L, SEQS, D), 1.0, 6.0, ((0, 4), (1, 8)))
    cotangent = scatter_about(seeds[1], (L, SEQS, D), 1.0, 6.0, ((0, 4), (1, 8)))
    gains = jnp.clip(1.0 + 0.1 * jax.random.normal(seeds[2], (2, D), jnp.float32), 0.5, 1.5)
    gain_first = scatter_about(seeds[3], (2, D), (0.077 * TOKENS ** 0.5), 54.3058, (), jnp.float32)
    gain_second = jnp.clip(jnp.exp(jax.random.uniform(seeds[4], (2, D), jnp.float32, math.log(11.239424), math.log(80.2816))), 11.239424, 80.2816)
    mix_logits = scatter_about(seeds[5], (H, L, L), 1.5, 9.0, ((2, 4),), jnp.float32)
    logit_first = draw_logit_first(jax.random.fold_in(seeds[20], 71), 0)
    logit_second = draw_logit_second(jax.random.fold_in(seeds[20], 71), 0)
    w_value = scatter_about(seeds[8], (D, D), D ** -0.5, 0.21875, ((0, 8),), jnp.float32)
    value_first = scatter_about(seeds[9], (D, D), (0.088 * TOKENS ** 0.5), 63.356766, ((0, 8),), jnp.float32)
    value_second = jnp.clip(jnp.exp(math.log(104.8576) - 1.9661128 * jax.random.uniform(seeds[10], (D, D), jnp.float32) ** block_scale(seeds[10], (D, D), ((0, 8),), -0.2, 0.2)), 14.680064, 104.8576)
    w_out = scatter_about(seeds[11], (D, D), (D * 16 // L) ** -0.5, 1.75, ((0, 8),), jnp.float32)
    out_first = scatter_about(seeds[12], (D, D), (0.11 * TOKENS ** 0.5 * min(0.8, 5.0 / L ** 0.5)), 12.44508, ((0, 8),), jnp.float32)
    out_second = jnp.clip(jnp.exp(math.log(4.0) - 1.9661129 * jax.random.uniform(seeds[13], (D, D), jnp.float32) ** block_scale(seeds[13], (D, D), ((0, 8),), -0.2, 0.2)), 0.56, 4.0)
    w_up = scatter_about(seeds[14], (D, FF), D ** -0.5, 0.21875, ((0, 8),), jnp.float32)
    up_first = scatter_about(seeds[15], (D, FF), (0.033 * TOKENS ** 0.5), 23.532515, ((0, 8),), jnp.float32)
    up_second = jnp.clip(jnp.exp(math.log(14.7456) - 1.9661128 * jax.random.uniform(seeds[16], (D, FF), jnp.float32) ** block_scale(seeds[16], (D, FF), ((0, 8),), -0.2, 0.2)), 2.064384, 14.7456)
    w_down = scatter_about(seeds[17], (FF, D), FF ** -0.5, 0.109375, ((0, 8),), jnp.float32)
    down_first = scatter_about(seeds[18], (FF, D), (0.066 * TOKENS ** 0.5), 47.06503, ((0, 8),), jnp.float32)
    down_second = jnp.clip(jnp.exp(math.log(58.9824) - 1.9661128 * jax.random.uniform(seeds[19], (FF, D), jnp.float32) ** block_scale(seeds[19], (FF, D), ((0, 8),), -0.2, 0.2)), 8.257536, 58.9824)
    return dict(tokens=tokens, cotangent=cotangent, gains=gains, gain_first=gain_first, gain_second=gain_second, mix_logits=mix_logits, logit_first=logit_first, logit_second=logit_second, w_value=w_value, value_first=value_first, value_second=value_second, w_out=w_out, out_first=out_first, out_second=out_second, w_up=w_up, up_first=up_first, up_second=up_second, w_down=w_down, down_first=down_first, down_second=down_second)


@jax.custom_vjp
def low(v):
    return lax.optimization_barrier(v.astype(jnp.bfloat16)).astype(jnp.float32)

@jax.custom_vjp
def low_back(v):
    return v

def low_keep(v):
    return (low(v), None)

def low_pass(kept, grad):
    return (grad,)

def back_keep(v):
    return (v, None)

def back_low(kept, grad):
    return (low(grad),)
low.defvjp(low_keep, low_pass)
low_back.defvjp(back_keep, back_low)
norm_eps = 1e-05
beta_first = 0.9
beta_second = 0.999
adam_eps = 1e-08
weight_decay = 0.1
hidden_floor = -1e+30

def matmul(left, right):
    return jnp.dot(left, right, precision=lax.Precision.HIGHEST, preferred_element_type=jnp.float32)

def normalize(hidden, gain):
    scale = lax.rsqrt(lax.optimization_barrier(jnp.mean(hidden * hidden, axis=-1, keepdims=True)) + norm_eps)
    return hidden * scale * gain

def gelu_tanh(inputs):
    return jax.nn.gelu(inputs, approximate=True)

def adam_update(weight, first, second, gradient, rate, decay):
    first_new = beta_first * first + (1.0 - beta_first) * gradient
    second_new = beta_second * second + (1.0 - beta_second) * gradient * gradient
    first_hat = first_new / (1.0 - beta_first ** STEP)
    second_hat = second_new / (1.0 - beta_second ** STEP)
    weight_new = weight - rate * (first_hat / (jnp.sqrt(second_hat) + adam_eps) + decay * weight)
    return (weight_new, first_new, second_new)

def layer_forward(tokens, gains, mix_logits, w_value, w_out, w_up, w_down):
    head_count, length, _ = mix_logits.shape
    width = tokens.shape[2]
    seq_total = tokens.shape[1]
    row_index = jnp.arange(length, dtype=jnp.int32)
    visible = (row_index[None, :] <= row_index[:, None])[None]
    masked = jnp.where(visible, mix_logits, hidden_floor)
    row_top = lax.optimization_barrier(jnp.max(masked, axis=-1, keepdims=True))
    expon = jnp.where(visible, jnp.exp(masked - row_top), 0.0)
    attention = low(expon / lax.optimization_barrier(jnp.sum(expon, axis=-1, keepdims=True)))
    value_w = low(w_value)
    out_w = low(w_out)
    up_w = low(w_up)
    down_w = low(w_down)
    group = math.gcd(seq_total, max(1, 4096 // length))
    groups = seq_total // group

    def group_fn(block):
        normed_in = low(normalize(block, gains[0]))
        values = low_back(low(matmul(normed_in, value_w)))
        values_heads = values.reshape(length, group, head_count, width // head_count)
        mixed = jnp.einsum('hij,jshc->ishc', attention, values_heads, precision=lax.Precision.HIGHEST)
        mixed = low_back(low(mixed.reshape(length, group, width)))
        hidden = block + low_back(matmul(mixed, out_w))
        normed_mid = low(normalize(hidden, gains[1]))
        up_pre = low_back(matmul(normed_mid, up_w))
        active = low(gelu_tanh(up_pre))
        return hidden + low_back(matmul(active, down_w))
    stacked = tokens.reshape(length, groups, group, width).transpose(1, 0, 2, 3)
    results = lax.map(jax.checkpoint(group_fn), stacked)
    return results.transpose(1, 0, 2, 3).reshape(length, seq_total, width)

def reference(tokens, cotangent, gains, gain_first, gain_second, mix_logits, logit_first, logit_second, w_value, value_first, value_second, w_out, out_first, out_second, w_up, up_first, up_second, w_down, down_first, down_second):
    output, pullback = jax.vjp(layer_forward, tokens.astype(jnp.float32), gains, mix_logits, w_value, w_out, w_up, w_down)
    grads = pullback(cotangent.astype(jnp.float32))
    input_grad, gain_grad, logit_grad, value_grad, out_grad, up_grad, down_grad = grads
    gains_new, gain_first_new, gain_second_new = adam_update(gains, gain_first, gain_second, gain_grad, 0.8, 0.0)
    logits_new, logit_first_new, logit_second_new = adam_update(mix_logits, logit_first, logit_second, logit_grad, 1.5, weight_decay)
    value_new, value_first_new, value_second_new = adam_update(w_value, value_first, value_second, value_grad, 1.0 / math.sqrt(D), weight_decay)
    out_new, out_first_new, out_second_new = adam_update(w_out, out_first, out_second, out_grad, 1.0 / math.sqrt(D * 16 // L), weight_decay)
    up_new, up_first_new, up_second_new = adam_update(w_up, up_first, up_second, up_grad, 1.0 / math.sqrt(D), weight_decay)
    down_new, down_first_new, down_second_new = adam_update(w_down, down_first, down_second, down_grad, 1.0 / math.sqrt(FF), weight_decay)
    return (output.astype(jnp.bfloat16), input_grad.astype(jnp.bfloat16), gains_new, gain_first_new, gain_second_new, logits_new, logit_first_new, logit_second_new, value_new, value_first_new, value_second_new, out_new, out_first_new, out_second_new, up_new, up_first_new, up_second_new, down_new, down_first_new, down_second_new)
```

```python
import functools
import math

import jax
import jax.numpy as jnp
from jax import lax
from jax.experimental import pallas as pl
from jax.experimental.pallas import tpu as pltpu
from jax.sharding import PartitionSpec as P

STEP = 10

norm_eps = 1e-05
beta_first = 0.9
beta_second = 0.999
adam_eps = 1e-08
weight_decay = 0.1
gelu_slope = math.sqrt(2.0 / math.pi)
gelu_cubic = 0.044715

BF = jnp.bfloat16
F32 = jnp.float32
VMEM = 60 * 1024 * 1024
PLAN = "mmuc0mb0i1p1vg2w2wgq3wgwgwg4w5"
LONG, SHORT, FRONT, UPDATE = 200,8,0.5,20
MIX0, MIX1, MIX2 = 200,200,200
GROUP_HEADS = (4, 4, 4)


def bits_of(size):
    return size.bit_length() - 1


def adam_update(weight, first, second, gradient, rate, decay):
    first_new = beta_first * first + (1.0 - beta_first) * gradient
    second_new = beta_second * second + (1.0 - beta_second) * gradient * gradient
    first_hat = first_new / (1.0 - beta_first**STEP)
    second_hat = second_new / (1.0 - beta_second**STEP)
    weight_new = weight - rate * (first_hat / (jnp.sqrt(second_hat) + adam_eps) + decay * weight)
    return (weight_new, first_new, second_new)


def swap(x, axis, mask):
    size = lax.axis_size(axis)
    return lax.ppermute(x, axis, [(i, i ^ mask) for i in range(size)])


def bit_value(axis, bit):
    return (lax.axis_index(axis) >> bit) & 1


def chip_bits(axis):
    return [(axis, b) for b in range(1, bits_of(lax.axis_size(axis)))]


def axis_rank(step):
    axis, bit = step
    return (0 if axis == "seq" else 1, -bit)


def nothing(*refs):
    pass


def behind(x, after, micros=SHORT):
    if not after:
        return x
    anywhere = pl.BlockSpec(memory_space=pl.ANY)
    return pl.pallas_call(
        nothing,
        in_specs=[anywhere] * (1 + len(after)),
        out_specs=anywhere,
        out_shape=jax.ShapeDtypeStruct(x.shape, x.dtype),
        input_output_aliases={0: 0},
        cost_estimate=cost(micros),
        name="behind",
    )(x, *after)


def run(function, *inputs, after=(), micros=SHORT):
    return function(behind(inputs[0], after, micros), *inputs[1:])


class Gather:
    def __init__(self, piece, steps, lead):
        self.out, self.steps, self.lead = piece, list(steps), lead
        self.done = []
        self.shape = (*piece.shape[:lead], -1, piece.shape[-1])
        self.start()

    def start(self):
        if self.steps:
            axis, bit = self.steps[0]
            self.got = swap(self.out, axis, 1 << bit)

    def next(self, after=(), micros=SHORT):
        step = self.steps.pop(0)
        place = self.lead + sum(1 for d in self.done if axis_rank(d) < axis_rank(step))
        high = bit_value(*step) == 1
        self.out = run(
            lambda got, out: jnp.where(
                high, jnp.stack([got, out], axis=place), jnp.stack([out, got], axis=place)
            ),
            self.got,
            self.out,
            after=after,
            micros=micros,
        )
        self.done.append(step)
        self.start()
        return self

    def result(self):
        return self.out.reshape(self.shape)


def bit_array(step):
    return bit_value(*step).astype(jnp.int32).reshape(1)


def halves_kernel(bit_ref, *refs):
    *ins, send_ref, keep_ref = refs
    total = ins[0][...].astype(F32)
    for ref in ins[1:]:
        total = total + ref[...].astype(F32)
    total = total.astype(BF)[:, 0]

    @pl.when(pl.program_id(0) == 0)
    def _():
        send_ref[...] = total

    @pl.when(pl.program_id(0) == 1)
    def _():
        keep_ref[...] = total


def halves_sum(terms, step):
    n, _, rows, columns = terms[0].shape
    blocks = 4 if n % 4 == 0 and n * rows * columns > 1 << 19 else 1
    size = n // blocks
    last = blocks - 1
    return pl.pallas_call(
        halves_kernel,
        grid_spec=pltpu.PrefetchScalarGridSpec(
            num_scalar_prefetch=1,
            grid=(2, blocks),
            in_specs=[
                pl.BlockSpec(
                    (size, 1, rows, columns), lambda i, j, bit: (j, bit[0] ^ (1 - i), 0, 0)
                )
            ]
            * len(terms),
            out_specs=[
                pl.BlockSpec((size, rows, columns), lambda i, j, _: (j * (1 - i) + last * i, 0, 0)),
                pl.BlockSpec((size, rows, columns), lambda i, j, _: (j * i, 0, 0)),
            ],
        ),
        out_shape=[jax.ShapeDtypeStruct((n, rows, columns), BF)] * 2,
        compiler_params=params(),
        cost_estimate=cost(SHORT),
        name="halves_sum",
    )(bit_array(step), *terms)


def sum_kernel(a_ref, b_ref, out_ref):
    out_ref[...] = (a_ref[...].astype(F32) + b_ref[...].astype(F32)).astype(BF)


def sum_of(a, b):
    return pl.pallas_call(
        sum_kernel,
        out_shape=jax.ShapeDtypeStruct(a.shape, BF),
        compiler_params=params(),
        cost_estimate=cost(SHORT),
        name="sum_of",
    )(a, b)


class HalvesOut:
    def __init__(self, send, keep, steps):
        self.steps = list(steps)
        self.columns = send.shape[-1]
        self.send, self.keep = (x.reshape(-1, self.columns) for x in (send, keep))
        self.trade()

    def trade(self):
        axis, bit = self.steps.pop(0)
        self.got = swap(self.send, axis, 1 << bit)

    def next(self, after):
        got = behind(self.got, after)
        terms = [x.reshape(1, 2, -1, self.columns) for x in (self.keep, got)]
        send, keep = halves_sum(terms, self.steps[0])
        self.send, self.keep = send[0], keep[0]
        self.trade()


def pieces_kernel(*refs):
    *ins, out_ref = refs
    for i in range(len(ins) // 2):
        total = ins[2 * i][...].astype(F32) + ins[2 * i + 1][...].astype(F32)
        out_ref[i] = total.astype(BF)


def pieces_of(pairs):
    rows, columns = pairs[0][0].shape
    half = pl.BlockSpec((rows // 2, columns), lambda i: (i, 0))
    return pl.pallas_call(
        pieces_kernel,
        grid=(2,),
        in_specs=[half] * (2 * len(pairs)),
        out_specs=pl.BlockSpec((len(pairs), rows // 2, columns), lambda i: (0, i, 0)),
        out_shape=jax.ShapeDtypeStruct((len(pairs), rows, columns), BF),
        compiler_params=params(),
        cost_estimate=cost(SHORT),
        name="pieces",
    )(*[x for pair in pairs for x in pair])


class RowSum:
    def __init__(self, keep, got, lead, steps, dims):
        self.keep, self.got, self.lead = keep, got, lead
        self.steps, self.left = list(steps), list(dims)
        self.columns = keep.shape[-1]

    def next(self, after):
        step = self.steps.pop(0)
        place = self.left.index(step)
        shape = (self.lead << place, 2, -1, self.columns)
        got = behind(self.got, after)
        send, self.keep = halves_sum([t.reshape(shape) for t in (self.keep, got)], step)
        axis, bit = step
        self.got = swap(send, axis, 1 << bit)
        self.left.remove(step)
        return send


def send_to_queries(blocks):
    size = lax.axis_size("pos")
    blocks = dict(enumerate(blocks))
    own = [blocks[0]]
    sent = None
    for bit in range(bits_of(size)):
        mask = 1 << bit
        for r in sorted((k for k in blocks if k & mask), reverse=True):
            pairs = [(p, p ^ mask) for p in range(size) if (p & ~(mask - 1)) <= (p ^ r)]
            sent = blocks.pop(r)
            got = lax.ppermute(sent, "pos", pairs)
            if r == mask:
                own.append(got)
            else:
                blocks[r ^ mask] = (blocks[r ^ mask].astype(F32) + got.astype(F32)).astype(BF)
    return own, sent


def gather_queries(own, bits, blocks=None):
    size = lax.axis_size("pos")
    blocks = dict(blocks or {0: own})
    for bit in bits:
        mask = 1 << bit
        for r in sorted(blocks):
            if r | mask in blocks:
                continue
            pairs = [
                (p ^ mask, p) for p in range(size) if (p & ~(mask - 1)) <= (p ^ r ^ mask)
            ]
            blocks[r | mask] = lax.ppermute(blocks[r], "pos", pairs)
    return blocks


def params():
    return pltpu.CompilerParams(vmem_limit_bytes=VMEM)


def cost(micros):
    return pl.CostEstimate(flops=int(micros * 1e9), bytes_accessed=0, transcendentals=0)


def column_of(table, index):
    lane = lax.broadcasted_iota(jnp.int32, table.shape, 1)
    return jnp.sum(jnp.where(lane == index, table, 0.0), axis=1, keepdims=True)


def lower(rows, columns):
    return lax.broadcasted_iota(jnp.int32, (rows, columns), 1) <= lax.broadcasted_iota(
        jnp.int32, (rows, columns), 0
    )


def dot(left, right, contract):
    return lax.dot_general(left, right, (contract, ((), ())), preferred_element_type=F32)


def totals_kernel(blocks, pos_ref, logits_ref, *refs):
    out_ref, acc_ref = refs[-2:]
    pair = pl.program_id(0)
    heads, length, width = logits_ref.shape
    me = pos_ref[0]

    @pl.when(pair == 0)
    def _():
        acc_ref[...] = jnp.zeros_like(acc_ref)

    lane = lax.broadcasted_iota(jnp.int32, (width, acc_ref.shape[1]), 1)
    for q in range(blocks):

        @pl.when(q >= me)
        def _(q=q):
            rows = pl.ds(q * width, width)
            acc = acc_ref[rows, :]
            for h in range(heads):
                e = jnp.exp(logits_ref[h, rows, :])
                e = jnp.where(lower(width, width) | (q > me), e, 0.0)
                acc = jnp.where(lane == pair * heads + h, jnp.sum(e, axis=1, keepdims=True), acc)
            acc_ref[rows, :] = acc

    @pl.when(pair == pl.num_programs(0) - 1)
    def _():
        out_ref[...] = acc_ref[...].T[:16]


def row_totals(pos, logits, blocks, after):
    heads, length, width = logits.shape
    return pl.pallas_call(
        functools.partial(totals_kernel, blocks),
        grid_spec=pltpu.PrefetchScalarGridSpec(
            num_scalar_prefetch=1,
            grid=(heads // 2,),
            in_specs=[pl.BlockSpec((2, length, width), lambda m, _: (m, 0, 0))]
            + [pl.BlockSpec(memory_space=pl.ANY)] * len(after),
            out_specs=pl.BlockSpec((16, length), lambda m, _: (0, 0)),
            scratch_shapes=[pltpu.VMEM((length, 128), F32)],
        ),
        out_shape=jax.ShapeDtypeStruct((16, length), F32),
        compiler_params=params(),
        cost_estimate=cost(FRONT),
        name="row_totals",
    )(pos, logits, *after)


def attention_kernel(blocks, pos_ref, logits_ref, scale_ref, out_ref):
    pair = pl.program_id(0)
    heads, length, width = logits_ref.shape
    me = pos_ref[0]
    for q in range(blocks):
        rows = pl.ds(q * width, width)

        @pl.when(q >= me)
        def _(rows=rows, q=q):
            scale = scale_ref[:, rows].T
            for h in range(heads):
                a = jnp.exp(logits_ref[h, rows, :]) * column_of(scale, pair * heads + h)
                a = jnp.where(lower(width, width) | (q > me), a, 0.0)
                out_ref[h, rows, :] = a.astype(BF)

        @pl.when(q < me)
        def _(rows=rows):
            for h in range(heads):
                out_ref[h, rows, :] = jnp.zeros((width, width), BF)


def attention_of(pos, logits, scale, blocks):
    heads, length, width = logits.shape
    pair = pl.BlockSpec((2, length, width), lambda m, _: (m, 0, 0))
    return pl.pallas_call(
        functools.partial(attention_kernel, blocks),
        grid_spec=pltpu.PrefetchScalarGridSpec(
            num_scalar_prefetch=1,
            grid=(heads // 2,),
            in_specs=[pair, pl.BlockSpec((16, length), lambda m, _: (0, 0))],
            out_specs=pair,
        ),
        out_shape=jax.ShapeDtypeStruct(logits.shape, BF),
        compiler_params=params(),
        cost_estimate=cost(FRONT),
        name="attention",
    )(pos, logits, scale)


def half_mask(rows, columns, half):
    lane = lax.broadcasted_iota(jnp.int32, (rows, columns), 1)
    return ((lane >> 6) & 1) == half


def split_heads(wide):
    zero = jnp.zeros_like(wide)
    first = half_mask(wide.shape[0], wide.shape[1], 0)
    return jnp.concatenate([jnp.where(first, wide, zero), jnp.where(first, zero, wide)], axis=0)


def forward_kernel(blocks, pos_ref, attention_ref, values_ref, *outs):
    *outs, all_ref = outs
    width = attention_ref.shape[2]
    seqs = values_ref.shape[0]
    me = pos_ref[0]
    values = split_heads(jnp.concatenate([values_ref[s] for s in range(seqs)], axis=1))
    both = jnp.concatenate([attention_ref[0], attention_ref[1]], axis=1)
    all_ref[...] = dot(both, values, ((1,), (0,))).astype(BF)
    for r in range(blocks):
        rows = pl.ds(pl.multiple_of((me ^ r) * width, width), width)
        for s in range(seqs):
            outs[r][s] = all_ref[rows, s * 128 : s * 128 + 128]


def mix_forward(pos, attention, values, blocks):
    heads, length, width = attention.shape
    seqs, _, wide = values.shape
    part = pl.BlockSpec((seqs, width, 128), lambda m, _: (0, 0, m))
    return pl.pallas_call(
        functools.partial(forward_kernel, blocks),
        grid_spec=pltpu.PrefetchScalarGridSpec(
            num_scalar_prefetch=1,
            grid=(heads // 2,),
            in_specs=[pl.BlockSpec((2, length, width), lambda m, _: (m, 0, 0)), part],
            out_specs=[part] * blocks,
            scratch_shapes=[pltpu.VMEM((length, seqs * 128), BF)],
        ),
        out_shape=[jax.ShapeDtypeStruct((seqs, width, wide), BF)] * blocks,
        compiler_params=params(),
        cost_estimate=cost(FRONT),
        name="mix_forward",
    )(pos, attention, values)


def ffn_kernel(parts, core_ref, *refs):
    (own_ref, got_ref, tokens_ref, cot_ref, gain_ref), refs = refs[:5], refs[5:]
    part_refs, refs = refs[:parts], refs[parts:]
    (
        output_ref,
        mixed_ref,
        normed_ref,
        active_ref,
        up_grad_ref,
        grad_hidden_ref,
        hidden_bf_ref,
        *group_refs,
        gain_grad_ref,
        wa,
        wb,
        product,
        sems,
    ) = refs
    step = pl.program_id(0)
    core = core_ref[0]
    half = own_ref.shape[-1]
    rows, width = tokens_ref.shape[1:]
    mine = pl.ds(pl.multiple_of(core * half, half), half)
    theirs = pl.ds(pl.multiple_of((1 - core) * half, half), half)

    @pl.when(step == 0)
    def _():
        copies = []
        for ref, lanes, sem in ((own_ref, mine, 0), (got_ref, theirs, 1)):
            for u in range(wa.shape[0]):
                copies.append((ref.at[:, u], wa.at[u, :, :, :, lanes], sems.at[sem, u]))
            for j in range(wb.shape[2]):
                u = wa.shape[0] + j
                copies.append((ref.at[:, u], wb.at[:, :, j, :, lanes], sems.at[sem, u]))
        copies = [pltpu.make_async_copy(*copy) for copy in copies]
        for copy in copies:
            copy.start()
        for copy in copies:
            copy.wait()
        product[...] = jnp.zeros_like(product)
        gain_grad_ref[...] = jnp.zeros_like(gain_grad_ref)
        for ref in group_refs:
            ref[...] = jnp.zeros_like(ref)

    w_out = wa[0].reshape(width, width)
    gain = gain_ref[...]
    mixed = part_refs[0][0].astype(F32)
    for ref in part_refs[1:]:
        mixed = mixed + ref[0].astype(F32)
    mixed = mixed.astype(BF)
    mixed_ref[0] = mixed
    hidden = tokens_ref[0].astype(F32) + dot(mixed, w_out, ((1,), (0,)))
    scale = lax.rsqrt(jnp.mean(hidden * hidden, axis=1, keepdims=True) + norm_eps)
    normed = (hidden * scale * gain).astype(BF)
    normed_ref[0] = normed
    cot = cot_ref[0]
    out = hidden
    grad_mid = jnp.zeros((rows, width), F32)
    for j in range(active_ref.shape[0]):
        if wb.shape[0] == 1:
            down = wb[0, 0, j]
        else:
            owners = wb.shape[0] // active_ref.shape[0]
            down = wb[j * owners : (j + 1) * owners].reshape(width, width)
        up = wa[1 + j].reshape(width, width)
        u = dot(normed, up, ((1,), (0,)))
        ga = dot(cot, down, ((1,), (1,)))
        square = u * u
        t = jnp.tanh(u * (gelu_slope + gelu_slope * gelu_cubic * square))
        plus = 0.5 + 0.5 * t
        active = (u * plus).astype(BF)
        slope = plus + (0.5 * u) * (1.0 - t * t) * (
            gelu_slope + 3.0 * gelu_slope * gelu_cubic * square
        )
        up_grad = (ga * slope).astype(BF)
        active_ref[j, 0] = active
        up_grad_ref[j, 0] = up_grad
        out = out + dot(active, down, ((1,), (0,)))
        grad_mid = grad_mid + dot(up_grad, up, ((1,), (1,)))
    output_ref[0] = out.astype(BF)
    gain_grad_ref[...] += jnp.sum(grad_mid * hidden * scale, axis=0, keepdims=True)
    weighted = grad_mid * gain
    inner = jnp.mean(weighted * hidden, axis=1, keepdims=True)
    grad_hidden = cot.astype(F32) + scale * weighted - hidden * (scale * scale * scale * inner)
    grad_hidden_ref[0] = grad_hidden
    hidden_bf = grad_hidden.astype(BF)
    hidden_bf_ref[0] = hidden_bf
    grad_mixed = dot(hidden_bf, w_out, ((1,), (1,))).astype(BF)
    place = pl.ds(pl.multiple_of(step * rows, rows), rows)
    cuts = []
    for ref in group_refs:
        first = cuts[-1].stop if cuts else 0
        cuts.append(slice(first, first + ref.shape[2]))
        ref[0, place, :] = grad_mixed[:, cuts[-1]]
    product[...] += grad_mixed.astype(F32) * mixed.astype(F32)

    @pl.when(step == pl.num_programs(0) - 1)
    def _():
        for ref, cut in zip(group_refs, cuts):
            lanes = cut.stop - cut.start
            head = lax.broadcasted_iota(jnp.int32, (8, lanes), 0)
            lane = lax.broadcasted_iota(jnp.int32, (8, lanes), 1)
            terms = lax.dot_general(
                jnp.where((lane >> 6) == head, 1.0, 0.0),
                product[:, cut],
                (((1,), (1,)), ((), ())),
                precision=lax.Precision.HIGHEST,
                preferred_element_type=F32,
            )
            ref[0, ref.shape[1] - 16 :, :rows] = two_parts(terms)


def two_parts(x):
    high = x.astype(BF).astype(F32)
    return jnp.concatenate([high, x - high], axis=0).astype(BF)


def one_part(x):
    count = x.shape[0] // 2
    x = x.astype(F32)
    return x[:count] + x[count:]


def feed_forward(core, own, got, tokens, cot, gain, parts, group_heads):
    seqs, rows, width = tokens.shape
    n_seq, units, chips, part_rows, _ = own.shape
    count = (units - 1) // 2
    act = pl.BlockSpec((1, rows, width), lambda s, _: (s, 0, 0))
    wide = pl.BlockSpec((count, 1, rows, width), lambda s, _: (0, s, 0, 0))
    payloads = [(1, seqs * rows + 16, 64 * heads) for heads in group_heads]
    anywhere = pl.BlockSpec(memory_space=pl.ANY)
    gain_spec = pl.BlockSpec((1, width), lambda s, _: (0, 0))
    act_bf = jax.ShapeDtypeStruct(tokens.shape, BF)
    wide_bf = jax.ShapeDtypeStruct((count, *tokens.shape), BF)
    tokens_all = seqs * rows
    return pl.pallas_call(
        functools.partial(ffn_kernel, len(parts)),
        grid_spec=pltpu.PrefetchScalarGridSpec(
            num_scalar_prefetch=1,
            grid=(seqs,),
            in_specs=[anywhere] * 2 + [act, act, gain_spec] + [act] * len(parts),
            out_specs=[act, act, act, wide, wide, act, act]
            + [pl.BlockSpec(payload, lambda s, _: (0, 0, 0)) for payload in payloads]
            + [gain_spec],
            scratch_shapes=[
                pltpu.VMEM((1 + count, n_seq, chips, part_rows, width), BF),
                pltpu.VMEM((n_seq, chips, count, part_rows, width), BF),
                pltpu.VMEM((rows, width), F32),
                pltpu.SemaphoreType.DMA((2, units)),
            ],
        ),
        out_shape=[act_bf] * 3
        + [wide_bf] * 2
        + [jax.ShapeDtypeStruct(tokens.shape, F32), act_bf]
        + [jax.ShapeDtypeStruct(payload, BF) for payload in payloads]
        + [jax.ShapeDtypeStruct((1, width), F32)],
        compiler_params=params(),
        cost_estimate=cost(SHORT),
        name="feed_forward",
    )(core, own, got, tokens, cot, gain, *parts)


def write_halves(core, grad, keep_ref, send_ref):
    half = keep_ref.shape[-1]
    for c in range(2):

        @pl.when(core == c)
        def _(c=c):
            keep_ref[0] = grad[:, c * half : c * half + half]
            send_ref[0] = grad[:, half - c * half : 2 * half - c * half]


def grads_kernel(first, core_ref, *refs):
    keep_ref, send_ref = refs[-2:]
    ins = refs[: 4 if first else 2]

    def write(left, right):
        grad = dot(
            left[...].reshape(left.shape[-2:]), right[...].reshape(right.shape[-2:]), ((0,), (0,))
        )
        write_halves(core_ref[0], grad.astype(BF), keep_ref, send_ref)

    if first:
        pl.when(pl.program_id(0) == 0)(lambda: write(ins[0], ins[1]))
        pl.when(pl.program_id(0) > 0)(lambda: write(ins[2], ins[3]))
    else:
        write(*ins)


def weight_grads(core, name, one, many, into=()):
    first = 1 if one else 0
    units = first + max(a.shape[0] for a in many if a.ndim == 3)
    rows, width = many[0].shape[-2:]

    def spec(a):
        if a.ndim == 2:
            return pl.BlockSpec((rows, width), lambda u, _: (0, 0))
        return pl.BlockSpec((1, rows, width), lambda u, _: (jnp.maximum(u - first, 0), 0, 0))

    ins = [*one, *many]
    out = pl.BlockSpec((1, width, width // 2), lambda u, _: (u, 0, 0))
    total = into[0].shape[0] if into else units
    return pl.pallas_call(
        functools.partial(grads_kernel, first),
        grid_spec=pltpu.PrefetchScalarGridSpec(
            num_scalar_prefetch=1,
            grid=(units,),
            in_specs=[spec(a) for a in ins] + [pl.BlockSpec(memory_space=pl.ANY)] * len(into),
            out_specs=[out, out],
        ),
        out_shape=[jax.ShapeDtypeStruct((total, width, width // 2), BF)] * 2,
        input_output_aliases={1 + len(ins) + i: i for i in range(len(into))},
        compiler_params=params(),
        cost_estimate=cost(SHORT),
        name=name,
    )(core, *ins, *into)


def pair_of(step, place_ref, split):
    return (1 - step) ^ place_ref[1] if split else step


def backward_kernel(blocks, split, place_ref, attention_ref, values_ref, *refs):
    grads, terms, refs = refs[:blocks], refs[blocks : 2 * blocks], refs[2 * blocks :]
    *outs, grad_values_ref, acc_ref, all_ref = refs
    step = pl.program_id(0)
    pair = pair_of(step, place_ref, split)
    _, length, width = attention_ref.shape
    seqs = values_ref.shape[0]
    me = place_ref[0]
    values = split_heads(jnp.concatenate([values_ref[s] for s in range(seqs)], axis=1))
    lane = lax.broadcasted_iota(jnp.int32, (width, 8), 1)

    for r in range(blocks):
        q = me ^ r

        @pl.when(q >= me)
        def _(r=r, q=q):
            rows = pl.ds(pl.multiple_of(q * width, width), width)
            grad = jnp.concatenate(
                [grads[r][0, s * width : (s + 1) * width, :] for s in range(seqs)], axis=1
            )
            scores = dot(grad, values, ((1,), (1,)))
            table = one_part(terms[r][0][:, :width]).T
            for h in range(2):
                term = jnp.sum(jnp.where(lane == pair * 2 + h, table, 0.0), axis=1, keepdims=True)
                a = attention_ref[h, rows, :].astype(F32)
                grad_a = (a * (scores[:, h * width : (h + 1) * width] - term)).astype(BF)
                all_ref[h, r] = grad_a
            part = dot(
                jnp.concatenate([attention_ref[0, rows, :], attention_ref[1, rows, :]], axis=0),
                split_heads(grad),
                ((0,), (0,)),
            )
            if r == 0:
                acc_ref[...] = part
            else:
                acc_ref[...] += part

        if r:

            @pl.when(q < me)
            def _(r=r):
                for h in range(2):
                    all_ref[h, r] = jnp.zeros((width, width), BF)

    if split:
        for i, out in enumerate(outs):

            @pl.when(step == i)
            def _(out=out):
                out[...] = all_ref[...]

    else:
        outs[0][...] = all_ref[...]

    total = acc_ref[...].astype(BF)
    for s in range(seqs):
        grad_values_ref[s] = total[:, s * 128 : s * 128 + 128]


def mix_backward(place, attention, values, grads, first, split):
    blocks = len(grads)
    _, length, width = attention.shape
    seqs = values.shape[0]
    lanes = grads[0].shape[2]
    pairs = lanes // 128
    before = first // 2

    def pair(m, at):
        return pair_of(m, at, split)

    part = pl.BlockSpec((1, seqs * width, 128), lambda m, at: (0, 0, pair(m, at)))
    terms = pl.BlockSpec((1, 16, lanes), lambda m, _: (0, seqs * width // 16, 0))
    out = pl.BlockSpec((2, blocks, width, width), lambda m, _: (0 if split else m, 0, 0, 0))
    outs = 2 if split else 1
    rows = 2 if split else 2 * pairs
    return pl.pallas_call(
        functools.partial(backward_kernel, blocks, split),
        grid_spec=pltpu.PrefetchScalarGridSpec(
            num_scalar_prefetch=1,
            grid=(pairs,),
            in_specs=[
                pl.BlockSpec((2, length, width), lambda m, at: (pair(m, at) + before, 0, 0)),
                pl.BlockSpec((seqs, width, 128), lambda m, at: (0, 0, pair(m, at) + before)),
            ]
            + [part] * blocks
            + [terms] * blocks,
            out_specs=[out] * outs
            + [pl.BlockSpec((seqs, width, 128), lambda m, at: (0, 0, pair(m, at)))],
            scratch_shapes=[
                pltpu.VMEM((width, seqs * 128), F32),
                pltpu.VMEM((2, blocks, width, width), BF),
            ],
        ),
        out_shape=[jax.ShapeDtypeStruct((rows, blocks, width, width), BF)] * outs
        + [jax.ShapeDtypeStruct((seqs, width, lanes), BF)],
        compiler_params=params(),
        cost_estimate=cost((MIX0, MIX1, MIX2)[first // 4 % 3]),
        name="mix_backward",
    )(place, attention, values, *grads, *grads)


def logits_adam_kernel(place_ref, weight_ref, first_ref, second_ref, *refs):
    grads, outs = refs[:4], refs[-3:]
    q = pl.program_id(1)
    me = place_ref[0]

    def update(h, gradient):
        weight = weight_ref[h]
        first = beta_first * first_ref[h]
        second = beta_second * second_ref[h]
        if gradient is not None:
            first = first + (1.0 - beta_first) * gradient
            second = second + ((1.0 - beta_second) * gradient) * gradient
        root = second * lax.rsqrt(second)
        bottom = root * math.sqrt(1.0 / (1.0 - beta_second**STEP)) + adam_eps
        step = first * (1.5 / (1.0 - beta_first**STEP)) / bottom
        outs[0][h] = weight * (1.0 - 1.5 * weight_decay) - step
        outs[1][h] = first
        outs[2][h] = second

    @pl.when(q >= me)
    def _():
        for h in range(4):
            update(h, grads[h][0, 0, 0].astype(F32))

    @pl.when(q < me)
    def _():
        for h in range(4):
            update(h, None)


def logits_adam(place, logits, first, second, pieces, group, start, before):
    heads, length, width = logits.shape
    blocks = length // width
    n_seq, groups, rows, _ = pieces.shape
    per = rows // width
    part = pl.BlockSpec((4, width, width), lambda k, q, _: (k + start // 4, q, 0))

    def owner(h, r):
        out = (h >> 1) + 2 * (h & 1)
        left, bit = blocks // 2, 4
        while left >= per:
            out = out + bit * ((r // left) % 2)
            left, bit = left // 2, bit * 2
        return out

    def grad(h):
        def index(k, q, at):
            r = jnp.where(q >= at[0], q ^ at[0], 0)
            return (owner(h, r), k + group, r % per, 0, 0)

        return pl.BlockSpec((1, 1, 1, width, width), index)

    ins = [logits, first, second] + [pieces.reshape(n_seq, groups, per, width, width)] * 4
    specs = [part] * 3 + [grad(h) for h in range(4)]
    aliases = {}
    if before is not None:
        aliases = {1 + len(ins) + i: i for i in range(3)}
        ins += list(before)
        specs += [pl.BlockSpec(memory_space=pl.ANY)] * 3
    return pl.pallas_call(
        logits_adam_kernel,
        grid_spec=pltpu.PrefetchScalarGridSpec(
            num_scalar_prefetch=1,
            grid=(1, blocks),
            in_specs=specs,
            out_specs=[part] * 3,
        ),
        out_shape=[jax.ShapeDtypeStruct(logits.shape, F32)] * 3,
        input_output_aliases=aliases,
        compiler_params=params(),
        cost_estimate=cost(UPDATE),
        name="logits_adam",
    )(place, *ins)


def input_kernel(groups, core_ref, *refs):
    grads, refs = refs[:groups], refs[groups:]
    (normed_ref, tokens_ref, value_ref, hidden_ref, gain_ref), refs = refs[:5], refs[5:]
    input_grad_ref, gain_grad_ref, keep_ref, send_ref, acc_ref = refs
    step = pl.program_id(0)
    grad = jnp.concatenate([ref[0] for ref in grads], axis=1)
    product = dot(normed_ref[0], grad, ((0,), (0,)))
    gain = gain_ref[...]
    tokens = tokens_ref[0].astype(F32)
    scale = lax.rsqrt(jnp.mean(tokens * tokens, axis=1, keepdims=True) + norm_eps)
    grad_in = dot(grad, value_ref[...], ((1,), (1,)))
    gain_part = jnp.sum(grad_in * tokens * scale, axis=0, keepdims=True)
    weighted = grad_in * gain
    inner = jnp.mean(weighted * tokens, axis=1, keepdims=True)
    total = hidden_ref[0] + scale * weighted - tokens * (scale * scale * scale * inner)
    input_grad_ref[0] = total.astype(BF)

    @pl.when(step == 0)
    def _():
        acc_ref[...] = product
        gain_grad_ref[...] = gain_part

    @pl.when(step > 0)
    def _():
        acc_ref[...] += product
        gain_grad_ref[...] += gain_part

    @pl.when(step == pl.num_programs(0) - 1)
    def _():
        write_halves(core_ref[0], acc_ref[...].astype(BF), keep_ref, send_ref)


def input_backward(core, grads, normed, tokens, value, hidden, gain):
    seqs, rows, width = tokens.shape
    act = pl.BlockSpec((1, rows, width), lambda s, _: (s, 0, 0))
    gain_spec = pl.BlockSpec((1, width), lambda s, _: (0, 0))
    half = pl.BlockSpec((1, width, width // 2), lambda s, _: (0, 0, 0))
    return pl.pallas_call(
        functools.partial(input_kernel, len(grads)),
        grid_spec=pltpu.PrefetchScalarGridSpec(
            num_scalar_prefetch=1,
            grid=(seqs,),
            in_specs=[
                pl.BlockSpec((1, rows, grad.shape[2]), lambda s, _: (s, 0, 0)) for grad in grads
            ]
            + [act, act, pl.BlockSpec((width, width), lambda s, _: (0, 0)), act, gain_spec],
            out_specs=[act, gain_spec, half, half],
            scratch_shapes=[pltpu.VMEM((width, width), F32)],
        ),
        out_shape=[
            jax.ShapeDtypeStruct(tokens.shape, BF),
            jax.ShapeDtypeStruct((1, width), F32),
            jax.ShapeDtypeStruct((1, width, width // 2), BF),
            jax.ShapeDtypeStruct((1, width, width // 2), BF),
        ],
        compiler_params=params(),
        cost_estimate=cost(SHORT),
        name="input_backward",
    )(core, *grads, normed, tokens, value, hidden, gain)


def bundle_kernel(keep_a, got_a, keep_b, got_b, out_ref):
    a = keep_a[...].astype(F32) + got_a[...].astype(F32)
    b = keep_b[...].astype(F32) + got_b[...].astype(F32)
    units = a.shape[0]
    out_ref[0, :units] = a[:, 0].astype(BF)
    out_ref[0, units:] = b[0].astype(BF)


def bundle(keep_a, got_a, keep_b, got_b):
    units, owners, rows, columns = keep_a.shape
    units_b = keep_b.shape[1]
    spec_a = pl.BlockSpec((units, 1, rows, columns), lambda g: (0, g, 0, 0))
    spec_b = pl.BlockSpec((1, units_b, rows, columns), lambda g: (g, 0, 0, 0))
    return pl.pallas_call(
        bundle_kernel,
        grid=(owners,),
        in_specs=[spec_a, spec_a, spec_b, spec_b],
        out_specs=pl.BlockSpec((1, units + units_b, rows, columns), lambda g: (g, 0, 0, 0)),
        out_shape=jax.ShapeDtypeStruct((owners, units + units_b, rows, columns), BF),
        compiler_params=params(),
        cost_estimate=cost(SHORT),
        name="bundle",
    )(keep_a, got_a, keep_b, got_b)


def merge_kernel(bit_ref, keep, got, value_keep, value_got, send_ref, keep_ref):
    value = (value_keep[:, 0].astype(F32) + value_got[:, 0].astype(F32)).astype(BF)
    others = (keep[:, 0].astype(F32) + got[:, 0].astype(F32)).astype(BF)
    for i, out in enumerate((send_ref, keep_ref)):

        @pl.when(pl.program_id(0) == i)
        def _(out=out):
            out[:, : others.shape[1]] = others
            out[:, others.shape[1] :] = value


def merge_halves(terms, step):
    n, _, units, rows, columns = terms[0].shape
    total = units + terms[2].shape[2]

    def spec(count):
        return pl.BlockSpec(
            (size, 1, count, rows, columns), lambda i, g, bit: (g, bit[0] ^ (1 - i), 0, 0, 0)
        )

    size = max(1, n // 4)
    last = n // size - 1
    block = (size, total, rows, columns)
    return pl.pallas_call(
        merge_kernel,
        grid_spec=pltpu.PrefetchScalarGridSpec(
            num_scalar_prefetch=1,
            grid=(2, n // size),
            in_specs=[spec(t.shape[2]) for t in terms],
            out_specs=[
                pl.BlockSpec(block, lambda i, g, _: (g * (1 - i) + last * i, 0, 0, 0)),
                pl.BlockSpec(block, lambda i, g, _: (g * i, 0, 0, 0)),
            ],
        ),
        out_shape=[jax.ShapeDtypeStruct((n, total, rows, columns), BF)] * 2,
        compiler_params=params(),
        cost_estimate=cost(SHORT),
        name="merge_halves",
    )(bit_array(step), *terms)


def whole_tiles(pieces, units):
    n_seq, _, chips, rows, half = pieces.shape
    a = pieces[:, : 1 + units].transpose(1, 0, 2, 3, 4)
    b = pieces[:, 1 + units :].transpose(0, 2, 1, 3, 4).reshape(units, -1, *a.shape[-1:])
    full = jnp.concatenate([a.reshape(1 + units, -1, half), b], axis=0)
    return full.reshape(1, 1 + 2 * units, 1, -1, half)


def body(
    tokens,
    cotangent,
    gains,
    gain_first,
    gain_second,
    mix_logits,
    logit_first,
    logit_second,
    w_value,
    value_first,
    value_second,
    w_out,
    out_first,
    out_second,
    w_up,
    up_first,
    up_second,
    w_down,
    down_first,
    down_second,
):
    head_count, length, width_pos = mix_logits.shape
    positions, seq_count, width = tokens.shape
    hidden_width = w_up.shape[1]
    token_rows = positions * seq_count
    units = hidden_width // width
    half = width // 2
    n_pos, n_seq = lax.axis_size("pos"), lax.axis_size("seq")
    pos = lax.axis_index("pos")
    pos_array = pos.astype(jnp.int32).reshape(1)
    place = jnp.stack([pos, bit_value("seq", 0)]).astype(jnp.int32)
    core = pos & 1
    core_array = core.astype(jnp.int32).reshape(1)
    chip = pos >> 1
    chips = n_pos // 2
    seq_low, pos_low = ("seq", 0), ("pos", 0)
    far = chip_bits("seq")
    across = chip_bits("pos")


    def own_piece(weight):
        rows, columns = weight.shape
        part = lax.dynamic_slice_in_dim(weight, chip * (rows // chips), rows // chips, 0)
        part = part.reshape(rows // chips, columns // width, 2, half)
        return lax.dynamic_index_in_dim(part, core, 2, keepdims=False).astype(BF)

    def both_halves(own, other):
        return jnp.where(
            core == 1,
            jnp.concatenate([other, own], axis=-1),
            jnp.concatenate([own, other], axis=-1),
        )

    away = far + across + [seq_low]
    value = Gather(own_piece(w_value)[:, 0], away, 0)
    part_rows = w_up.shape[0] // chips

    def other_pieces(out, up, down):
        a = jnp.concatenate([own_piece(out), own_piece(up)], axis=1).transpose(1, 0, 2)
        return jnp.concatenate([a, own_piece(down).reshape(units, part_rows, half)], axis=0)

    others = Gather(behind(other_pieces(w_out, w_up, w_down), (value.out,), LONG), across, 1)
    totals = row_totals(pos_array, mix_logits, n_pos, (value.out, others.out))
    totals_got = swap(totals, "pos", 1)
    for _ in across:
        others.next()
    others = others.result()
    last = others
    others = lax.all_gather(others, "seq", axis=0, tiled=False)

    tokens_rows, cot_rows = tokens.transpose(1, 0, 2), cotangent.transpose(1, 0, 2)
    tokens_wide = tokens_rows.reshape(token_rows, width).astype(F32)
    in_scale = lax.rsqrt(jnp.mean(tokens_wide * tokens_wide, axis=-1, keepdims=True) + norm_eps)
    normed_in = (tokens_wide * in_scale * gains[0]).astype(BF)
    for _ in far[1:]:
        value.next((last, totals), 1)
    for _, bit in across:
        totals = behind(totals_got, (value.out,), 1) + totals
        totals_got = swap(totals, "pos", 1 << bit)
    value.next((totals,), 1)
    for _ in across:
        value.next((normed_in,), 1)
    scale = 1.0 / (behind(totals_got, (value.out,), 1) + totals)
    attention = attention_of(pos_array, mix_logits, scale, n_pos)
    value.next((attention,), 1)
    value_half = value.result()
    value_other = swap(value_half, "pos", 1)
    value_full = both_halves(value_half, value_other)
    values = jnp.dot(normed_in, value_full, preferred_element_type=F32).astype(BF)
    values = values.reshape(seq_count, positions, width)
    parts, sent = send_to_queries(mix_forward(pos_array, attention, values, n_pos))
    others = behind(others, (sent,), 1).reshape(n_seq, 1 + 2 * units, chips, part_rows, half)
    if part_rows % 16:
        others = whole_tiles(others, units)
    others_got = swap(others, "pos", 1)
    parts[-1] = behind(parts[-1], (others,), LONG)
    (
        output,
        mixed,
        normed_mid,
        active,
        up_grad,
        grad_hidden,
        hidden_bf,
        *payloads,
        gain_mid,
    ) = feed_forward(
        core_array,
        others,
        others_got,
        tokens_rows,
        cot_rows,
        gains[1:2],
        parts,
        GROUP_HEADS,
    )

    def placed(x):
        return x.transpose(1, 0, 2)

    def rows_of(x):
        return x.reshape(*x.shape[:-3], token_rows, width)

    near = [gather_queries(part, [0])[1] for part in payloads]
    arrived = [gather_queries(part, [b for _, b in reversed(across)]) for part in payloads]
    keep_b, send_b = weight_grads(
        core_array, "grads_down", (), (rows_of(active), rows_of(cot_rows))
    )
    last = keep_b
    chains, grad_values = [], []
    keep_a = send_a = got_a = got_b = keep_w = got_w = value_terms = None
    chain = chain_a = chain_b = merged = owned = gain_total = input_grad = logits_out = None
    gain_steps = [pos_low] + across + far + [seq_low]

    def mixing_step():
        nonlocal last
        k = len(chains)
        for r in arrived[k]:
            if r:
                arrived[k][r] = behind(arrived[k][r], (last,), SHORT)
        blocks = gather_queries(None, [0], {**arrived[k], 1: near[k]})
        send, keep, grad_values_k = mix_backward(
            place,
            attention,
            values,
            [blocks[r] for r in range(n_pos)],
            sum(GROUP_HEADS[:k]),
            True,
        )
        grad_values.append(grad_values_k)
        chains.append(HalvesOut(send, keep, [seq_low] + far))
        last = send

    def grads_step():
        nonlocal keep_a, send_a, last
        keep_a, send_a = weight_grads(
            core_array,
            "grads_others",
            (rows_of(mixed), rows_of(hidden_bf)),
            (rows_of(normed_mid), behind(rows_of(up_grad), (last,), SHORT)),
        )
        last = keep_a

    def core_step():
        nonlocal got_a, got_b, last
        last = behind(send_a, (last,), SHORT)
        got_a, got_b = swap(last, "pos", 1), swap(send_b, "pos", 1)

    def input_step():
        nonlocal input_grad, gain_total, value_terms, last
        input_grad, gain_in, keep, send = input_backward(
            core_array,
            [behind(grad_values[0], (last,), SHORT), *grad_values[1:]],
            normed_in.reshape(tokens_rows.shape),
            tokens_rows,
            value_full,
            grad_hidden,
            gains[0:1],
        )
        gain_total = jnp.concatenate([gain_in, gain_mid], axis=0)
        value_terms = [keep, swap(send, "pos", 1)]
        last = keep

    def value_step():
        nonlocal value_terms, last
        value_terms[1] = behind(value_terms[1], (last,))
        for step in across:
            views = [t.reshape(-1, 2, part_rows, half) for t in value_terms]
            last, keep = halves_sum(views, step)
            value_terms = [keep, swap(last, "pos", 1 << step[1])]

    def bundle_step():
        nonlocal chain_a, chain_b, last
        dims = list(reversed(far)) + [seq_low] + list(reversed(across))
        chain_a = RowSum(keep_a, got_a, 1 + units, across + [seq_low], dims)
        chain_b = RowSum(keep_b.reshape(-1, half), got_b.reshape(-1, half), 1, across, dims)
        for _ in across:
            last = chain_a.next((last,))
        for _ in across:
            last = chain_b.next((last,))

    def projections_step():
        nonlocal chain, merged, owned, last
        owners = n_seq // 2
        if chain_a.steps:
            last = chain_a.next((last,))
        elif merged is None:
            shape = (owners, 2, -1, part_rows, half)
            terms = [
                x.reshape(shape)
                for x in (chain_b.keep, behind(chain_b.got, (last,)), *value_terms)
            ]
            last, keep = merge_halves(terms, seq_low)
            merged = [keep, swap(last, "seq", 1)]
        elif chain is None:
            a = [t.reshape(1 + units, owners, part_rows, half) for t in (chain_a.keep, chain_a.got)]
            b = [t.reshape(owners, 1 + units, part_rows, half) for t in merged]
            b[1] = behind(b[1], (last,))
            total = bundle(*a, *b)
            steps = list(far)
            step = steps.pop(0)
            left = [d for d in reversed(far)]
            view = total.reshape(1 << left.index(step), 2, -1, half)
            last, keep = halves_sum([view], step)
            left.remove(step)
            chain = RowSum(keep.reshape(-1, half), None, 1, steps, left)
            chain.got = swap(last, "seq", 1 << step[1]).reshape(-1, half)
        elif chain.steps:
            last = chain.next((last, placed(output), placed(input_grad)))
        elif owned is None:
            keep, got = (t.reshape(-1, half) for t in (chain.keep, chain.got))
            last = sum_of(keep, behind(got, (last,)))
            owned = Gather(last.reshape(2 + 2 * units, part_rows, half), list(reversed(across)), 1)
        elif owned.steps:
            owned.next((last,))
            last = owned.out

    def gain_step():
        nonlocal gain_total, last
        if gain_steps:
            axis, bit = gain_steps.pop(0)
            last = gain_total = behind(gain_total, (last,))
            gain_total = gain_total + swap(gain_total, axis, 1 << bit)

    def sum_step(k):
        nonlocal last
        if chains[k].steps:
            chains[k].next((last,))
            last = chains[k].send

    def gather_step(groups):
        nonlocal last
        for k in groups:
            while chains[k].steps:
                sum_step(k)
        pairs = [(chains[k].keep, chains[k].got) for k in groups]
        pairs[0] = (pairs[0][0], behind(pairs[0][1], (last,)))
        last = pieces_of(pairs)
        gathered[groups[0]] = lax.all_gather(last, "seq", axis=0, tiled=False)

    def update(k):
        nonlocal logits_out, last
        groups = next(g for g in parts_of if k in g)
        if groups[0] not in gathered:
            gather_step(groups)
        if k == groups[0]:
            gathered[groups[0]] = behind(gathered[groups[0]], (last,))
        logits_out = logits_adam(
            place,
            mix_logits,
            logit_first,
            logit_second,
            gathered[groups[0]],
            k - groups[0],
            sum(GROUP_HEADS[:k]),
            logits_out,
        )
        last = logits_out[0]

    steps = {
        "m": mixing_step,
        "u": grads_step,
        "c": core_step,
        "b": bundle_step,
        "w": projections_step,
        "i": input_step,
        "v": value_step,
        "g": gain_step,
    }
    for k in range(len(GROUP_HEADS)):
        steps[str(k)] = functools.partial(sum_step, k)
    gathered = {}
    parts_of = [0], list(range(1, len(GROUP_HEADS)))
    for name, k in zip("pq", parts_of):
        steps[name] = functools.partial(gather_step, k)
    for k in range(len(GROUP_HEADS)):
        steps[str(k + 3)] = functools.partial(update, k)
    for name in PLAN:
        steps[name]()
    while gain_steps:
        gain_step()
    while owned is None or owned.steps:
        projections_step()
    logits_new, logit_first_new, logit_second_new = logits_out
    owned = owned.result()
    owned = both_halves(owned, swap(owned, "pos", 1)).astype(F32)
    grad_out, grad_value = owned[0], owned[1 + 2 * units]
    grad_up = jnp.concatenate([owned[1 + j] for j in range(units)], axis=1)
    grad_down = owned[1 + units : 1 + 2 * units].reshape(units, chips, part_rows, width)
    grad_down = grad_down.transpose(1, 0, 2, 3).reshape(-1, width)
    gains_new, gain_first_new, gain_second_new = adam_update(
        gains, gain_first, gain_second, gain_total, 0.8, 0.0
    )
    value_new, value_first_new, value_second_new = adam_update(
        w_value, value_first, value_second, grad_value, 1.0 / math.sqrt(width), weight_decay
    )
    out_new, out_first_new, out_second_new = adam_update(
        w_out,
        out_first,
        out_second,
        grad_out,
        1.0 / math.sqrt(width * 16 // length),
        weight_decay,
    )
    up_new, up_first_new, up_second_new = adam_update(
        w_up, up_first, up_second, grad_up, 1.0 / math.sqrt(width), weight_decay
    )
    down_new, down_first_new, down_second_new = adam_update(
        w_down, down_first, down_second, grad_down, 1.0 / math.sqrt(hidden_width), weight_decay
    )
    return (
        placed(output),
        placed(input_grad),
        gains_new,
        gain_first_new,
        gain_second_new,
        logits_new,
        logit_first_new,
        logit_second_new,
        value_new,
        value_first_new,
        value_second_new,
        out_new,
        out_first_new,
        out_second_new,
        up_new,
        up_first_new,
        up_second_new,
        down_new,
        down_first_new,
        down_second_new,
    )


def solution(mesh):
    activations = P("pos", "seq", None)
    logits = P(None, None, "pos")
    rows = P("seq", None)
    placed = (activations,) * 2 + (P(),) * 3 + (logits,) * 3 + (rows,) * 12
    return jax.shard_map(
        body, mesh=mesh, in_specs=placed, out_specs=placed, check_vma=False
    )
```

```python
import functools
import math

import jax
import jax.numpy as jnp
from jax import lax
from jax.experimental import pallas as pl
from jax.experimental.pallas import tpu as pltpu
from jax.sharding import PartitionSpec as P

STEP = 10

norm_eps = 1e-05
beta_first = 0.9
beta_second = 0.999
adam_eps = 1e-08
weight_decay = 0.1
gelu_slope = math.sqrt(2.0 / math.pi)
gelu_cubic = 0.044715

BF = jnp.bfloat16
F32 = jnp.float32
VMEM = 60 * 1024 * 1024
PLAN = "mmuc0mb0i1p1vg2w2wgq3wgwgwg4w5"
LONG, SHORT, FRONT, UPDATE = 200,8,0.5,20
MIX0, MIX1, MIX2 = 200,200,200
GROUP_HEADS = (4, 4, 4)


def bits_of(size):
    return size.bit_length() - 1


def adam_update(weight, first, second, gradient, rate, decay):
    first_new = beta_first * first + (1.0 - beta_first) * gradient
    second_new = beta_second * second + (1.0 - beta_second) * gradient * gradient
    first_hat = first_new / (1.0 - beta_first**STEP)
    second_hat = second_new / (1.0 - beta_second**STEP)
    weight_new = weight - rate * (first_hat / (jnp.sqrt(second_hat) + adam_eps) + decay * weight)
    return (weight_new, first_new, second_new)


def swap(x, axis, mask):
    size = lax.axis_size(axis)
    return lax.ppermute(x, axis, [(i, i ^ mask) for i in range(size)])


def bit_value(axis, bit):
    return (lax.axis_index(axis) >> bit) & 1


def chip_bits(axis):
    return [(axis, b) for b in range(1, bits_of(lax.axis_size(axis)))]


def axis_rank(step):
    axis, bit = step
    return (0 if axis == "seq" else 1, -bit)


def nothing(*refs):
    pass


def behind(x, after, micros=SHORT):
    if not after:
        return x
    anywhere = pl.BlockSpec(memory_space=pl.ANY)
    return pl.pallas_call(
        nothing,
        in_specs=[anywhere] * (1 + len(after)),
        out_specs=anywhere,
        out_shape=jax.ShapeDtypeStruct(x.shape, x.dtype),
        input_output_aliases={0: 0},
        cost_estimate=cost(micros),
        name="behind",
    )(x, *after)


def run(function, *inputs, after=(), micros=SHORT):
    return function(behind(inputs[0], after, micros), *inputs[1:])


class Gather:
    def __init__(self, piece, steps, lead):
        self.out, self.steps, self.lead = piece, list(steps), lead
        self.done = []
        self.shape = (*piece.shape[:lead], -1, piece.shape[-1])
        self.start()

    def start(self):
        if self.steps:
            axis, bit = self.steps[0]
            self.got = swap(self.out, axis, 1 << bit)

    def next(self, after=(), micros=SHORT):
        step = self.steps.pop(0)
        place = self.lead + sum(1 for d in self.done if axis_rank(d) < axis_rank(step))
        high = bit_value(*step) == 1
        self.out = run(
            lambda got, out: jnp.where(
                high, jnp.stack([got, out], axis=place), jnp.stack([out, got], axis=place)
            ),
            self.got,
            self.out,
            after=after,
            micros=micros,
        )
        self.done.append(step)
        self.start()
        return self

    def result(self):
        return self.out.reshape(self.shape)


def bit_array(step):
    return bit_value(*step).astype(jnp.int32).reshape(1)


def halves_kernel(bit_ref, *refs):
    *ins, send_ref, keep_ref = refs
    total = ins[0][...].astype(F32)
    for ref in ins[1:]:
        total = total + ref[...].astype(F32)
    total = total.astype(BF)[:, 0]

    @pl.when(pl.program_id(0) == 0)
    def _():
        send_ref[...] = total

    @pl.when(pl.program_id(0) == 1)
    def _():
        keep_ref[...] = total


def halves_sum(terms, step):
    n, _, rows, columns = terms[0].shape
    blocks = 4 if n % 4 == 0 and n * rows * columns > 1 << 19 else 1
    size = n // blocks
    last = blocks - 1
    return pl.pallas_call(
        halves_kernel,
        grid_spec=pltpu.PrefetchScalarGridSpec(
            num_scalar_prefetch=1,
            grid=(2, blocks),
            in_specs=[
                pl.BlockSpec(
                    (size, 1, rows, columns), lambda i, j, bit: (j, bit[0] ^ (1 - i), 0, 0)
                )
            ]
            * len(terms),
            out_specs=[
                pl.BlockSpec((size, rows, columns), lambda i, j, _: (j * (1 - i) + last * i, 0, 0)),
                pl.BlockSpec((size, rows, columns), lambda i, j, _: (j * i, 0, 0)),
            ],
        ),
        out_shape=[jax.ShapeDtypeStruct((n, rows, columns), BF)] * 2,
        compiler_params=params(),
        cost_estimate=cost(SHORT),
        name="halves_sum",
    )(bit_array(step), *terms)


def sum_kernel(a_ref, b_ref, out_ref):
    out_ref[...] = (a_ref[...].astype(F32) + b_ref[...].astype(F32)).astype(BF)


def sum_of(a, b):
    return pl.pallas_call(
        sum_kernel,
        out_shape=jax.ShapeDtypeStruct(a.shape, BF),
        compiler_params=params(),
        cost_estimate=cost(SHORT),
        name="sum_of",
    )(a, b)


class HalvesOut:
    def __init__(self, send, keep, steps):
        self.steps = list(steps)
        self.columns = send.shape[-1]
        self.send, self.keep = (x.reshape(-1, self.columns) for x in (send, keep))
        self.trade()

    def trade(self):
        axis, bit = self.steps.pop(0)
        self.got = swap(self.send, axis, 1 << bit)

    def next(self, after):
        got = behind(self.got, after)
        terms = [x.reshape(1, 2, -1, self.columns) for x in (self.keep, got)]
        send, keep = halves_sum(terms, self.steps[0])
        self.send, self.keep = send[0], keep[0]
        self.trade()


def pieces_kernel(*refs):
    *ins, out_ref = refs
    for i in range(len(ins) // 2):
        total = ins[2 * i][...].astype(F32) + ins[2 * i + 1][...].astype(F32)
        out_ref[i] = total.astype(BF)


def pieces_of(pairs):
    rows, columns = pairs[0][0].shape
    half = pl.BlockSpec((rows // 2, columns), lambda i: (i, 0))
    return pl.pallas_call(
        pieces_kernel,
        grid=(2,),
        in_specs=[half] * (2 * len(pairs)),
        out_specs=pl.BlockSpec((len(pairs), rows // 2, columns), lambda i: (0, i, 0)),
        out_shape=jax.ShapeDtypeStruct((len(pairs), rows, columns), BF),
        compiler_params=params(),
        cost_estimate=cost(SHORT),
        name="pieces",
    )(*[x for pair in pairs for x in pair])


class RowSum:
    def __init__(self, keep, got, lead, steps, dims):
        self.keep, self.got, self.lead = keep, got, lead
        self.steps, self.left = list(steps), list(dims)
        self.columns = keep.shape[-1]

    def next(self, after):
        step = self.steps.pop(0)
        place = self.left.index(step)
        shape = (self.lead << place, 2, -1, self.columns)
        got = behind(self.got, after)
        send, self.keep = halves_sum([t.reshape(shape) for t in (self.keep, got)], step)
        axis, bit = step
        self.got = swap(send, axis, 1 << bit)
        self.left.remove(step)
        return send


def send_to_queries(blocks):
    size = lax.axis_size("pos")
    blocks = dict(enumerate(blocks))
    own = [blocks[0]]
    sent = None
    for bit in range(bits_of(size)):
        mask = 1 << bit
        for r in sorted((k for k in blocks if k & mask), reverse=True):
            pairs = [(p, p ^ mask) for p in range(size) if (p & ~(mask - 1)) <= (p ^ r)]
            sent = blocks.pop(r)
            got = lax.ppermute(sent, "pos", pairs)
            if r == mask:
                own.append(got)
            else:
                blocks[r ^ mask] = (blocks[r ^ mask].astype(F32) + got.astype(F32)).astype(BF)
    return own, sent


def gather_queries(own, bits, blocks=None):
    size = lax.axis_size("pos")
    blocks = dict(blocks or {0: own})
    for bit in bits:
        mask = 1 << bit
        for r in sorted(blocks):
            if r | mask in blocks:
                continue
            pairs = [
                (p ^ mask, p) for p in range(size) if (p & ~(mask - 1)) <= (p ^ r ^ mask)
            ]
            blocks[r | mask] = lax.ppermute(blocks[r], "pos", pairs)
    return blocks


def params():
    return pltpu.CompilerParams(vmem_limit_bytes=VMEM)


def cost(micros):
    return pl.CostEstimate(flops=int(micros * 1e9), bytes_accessed=0, transcendentals=0)


def column_of(table, index):
    lane = lax.broadcasted_iota(jnp.int32, table.shape, 1)
    return jnp.sum(jnp.where(lane == index, table, 0.0), axis=1, keepdims=True)


def lower(rows, columns):
    return lax.broadcasted_iota(jnp.int32, (rows, columns), 1) <= lax.broadcasted_iota(
        jnp.int32, (rows, columns), 0
    )


def dot(left, right, contract):
    return lax.dot_general(left, right, (contract, ((), ())), preferred_element_type=F32)


def totals_kernel(blocks, pos_ref, logits_ref, *refs):
    out_ref, acc_ref = refs[-2:]
    pair = pl.program_id(0)
    heads, length, width = logits_ref.shape
    me = pos_ref[0]

    @pl.when(pair == 0)
    def _():
        acc_ref[...] = jnp.zeros_like(acc_ref)

    lane = lax.broadcasted_iota(jnp.int32, (width, acc_ref.shape[1]), 1)
    for q in range(blocks):

        @pl.when(q >= me)
        def _(q=q):
            rows = pl.ds(q * width, width)
            acc = acc_ref[rows, :]
            for h in range(heads):
                e = jnp.exp(logits_ref[h, rows, :])
                e = jnp.where(lower(width, width) | (q > me), e, 0.0)
                acc = jnp.where(lane == pair * heads + h, jnp.sum(e, axis=1, keepdims=True), acc)
            acc_ref[rows, :] = acc

    @pl.when(pair == pl.num_programs(0) - 1)
    def _():
        out_ref[...] = acc_ref[...].T[:16]


def row_totals(pos, logits, blocks, after):
    heads, length, width = logits.shape
    return pl.pallas_call(
        functools.partial(totals_kernel, blocks),
        grid_spec=pltpu.PrefetchScalarGridSpec(
            num_scalar_prefetch=1,
            grid=(heads // 2,),
            in_specs=[pl.BlockSpec((2, length, width), lambda m, _: (m, 0, 0))]
            + [pl.BlockSpec(memory_space=pl.ANY)] * len(after),
            out_specs=pl.BlockSpec((16, length), lambda m, _: (0, 0)),
            scratch_shapes=[pltpu.VMEM((length, 128), F32)],
        ),
        out_shape=jax.ShapeDtypeStruct((16, length), F32),
        compiler_params=params(),
        cost_estimate=cost(FRONT),
        name="row_totals",
    )(pos, logits, *after)


def attention_kernel(blocks, pos_ref, logits_ref, scale_ref, out_ref):
    pair = pl.program_id(0)
    heads, length, width = logits_ref.shape
    me = pos_ref[0]
    for q in range(blocks):
        rows = pl.ds(q * width, width)

        @pl.when(q >= me)
        def _(rows=rows, q=q):
            scale = scale_ref[:, rows].T
            for h in range(heads):
                a = jnp.exp(logits_ref[h, rows, :]) * column_of(scale, pair * heads + h)
                a = jnp.where(lower(width, width) | (q > me), a, 0.0)
                out_ref[h, rows, :] = a.astype(BF)

        @pl.when(q < me)
        def _(rows=rows):
            for h in range(heads):
                out_ref[h, rows, :] = jnp.zeros((width, width), BF)


def attention_of(pos, logits, scale, blocks):
    heads, length, width = logits.shape
    pair = pl.BlockSpec((2, length, width), lambda m, _: (m, 0, 0))
    return pl.pallas_call(
        functools.partial(attention_kernel, blocks),
        grid_spec=pltpu.PrefetchScalarGridSpec(
            num_scalar_prefetch=1,
            grid=(heads // 2,),
            in_specs=[pair, pl.BlockSpec((16, length), lambda m, _: (0, 0))],
            out_specs=pair,
        ),
        out_shape=jax.ShapeDtypeStruct(logits.shape, BF),
        compiler_params=params(),
        cost_estimate=cost(FRONT),
        name="attention",
    )(pos, logits, scale)


def half_mask(rows, columns, half):
    lane = lax.broadcasted_iota(jnp.int32, (rows, columns), 1)
    return ((lane >> 6) & 1) == half


def split_heads(wide):
    zero = jnp.zeros_like(wide)
    first = half_mask(wide.shape[0], wide.shape[1], 0)
    return jnp.concatenate([jnp.where(first, wide, zero), jnp.where(first, zero, wide)], axis=0)


def forward_kernel(blocks, pos_ref, attention_ref, values_ref, *outs):
    *outs, all_ref = outs
    width = attention_ref.shape[2]
    seqs = values_ref.shape[0]
    me = pos_ref[0]
    values = split_heads(jnp.concatenate([values_ref[s] for s in range(seqs)], axis=1))
    both = jnp.concatenate([attention_ref[0], attention_ref[1]], axis=1)
    all_ref[...] = dot(both, values, ((1,), (0,))).astype(BF)
    for r in range(blocks):
        rows = pl.ds(pl.multiple_of((me ^ r) * width, width), width)
        for s in range(seqs):
            outs[r][s] = all_ref[rows, s * 128 : s * 128 + 128]


def mix_forward(pos, attention, values, blocks):
    heads, length, width = attention.shape
    seqs, _, wide = values.shape
    part = pl.BlockSpec((seqs, width, 128), lambda m, _: (0, 0, m))
    return pl.pallas_call(
        functools.partial(forward_kernel, blocks),
        grid_spec=pltpu.PrefetchScalarGridSpec(
            num_scalar_prefetch=1,
            grid=(heads // 2,),
            in_specs=[pl.BlockSpec((2, length, width), lambda m, _: (m, 0, 0)), part],
            out_specs=[part] * blocks,
            scratch_shapes=[pltpu.VMEM((length, seqs * 128), BF)],
        ),
        out_shape=[jax.ShapeDtypeStruct((seqs, width, wide), BF)] * blocks,
        compiler_params=params(),
        cost_estimate=cost(FRONT),
        name="mix_forward",
    )(pos, attention, values)


def ffn_kernel(parts, core_ref, *refs):
    (own_ref, got_ref, tokens_ref, cot_ref, gain_ref), refs = refs[:5], refs[5:]
    part_refs, refs = refs[:parts], refs[parts:]
    (
        output_ref,
        mixed_ref,
        normed_ref,
        active_ref,
        up_grad_ref,
        grad_hidden_ref,
        hidden_bf_ref,
        *group_refs,
        gain_grad_ref,
        wa,
        wb,
        product,
        sems,
    ) = refs
    step = pl.program_id(0)
    core = core_ref[0]
    half = own_ref.shape[-1]
    rows, width = tokens_ref.shape[1:]
    mine = pl.ds(pl.multiple_of(core * half, half), half)
    theirs = pl.ds(pl.multiple_of((1 - core) * half, half), half)

    @pl.when(step == 0)
    def _():
        copies = []
        for ref, lanes, sem in ((own_ref, mine, 0), (got_ref, theirs, 1)):
            for u in range(wa.shape[0]):
                copies.append((ref.at[:, u], wa.at[u, :, :, :, lanes], sems.at[sem, u]))
            for j in range(wb.shape[2]):
                u = wa.shape[0] + j
                copies.append((ref.at[:, u], wb.at[:, :, j, :, lanes], sems.at[sem, u]))
        copies = [pltpu.make_async_copy(*copy) for copy in copies]
        for copy in copies:
            copy.start()
        for copy in copies:
            copy.wait()
        product[...] = jnp.zeros_like(product)
        gain_grad_ref[...] = jnp.zeros_like(gain_grad_ref)
        for ref in group_refs:
            ref[...] = jnp.zeros_like(ref)

    w_out = wa[0].reshape(width, width)
    gain = gain_ref[...]
    mixed = part_refs[0][0].astype(F32)
    for ref in part_refs[1:]:
        mixed = mixed + ref[0].astype(F32)
    mixed = mixed.astype(BF)
    mixed_ref[0] = mixed
    hidden = tokens_ref[0].astype(F32) + dot(mixed, w_out, ((1,), (0,)))
    scale = lax.rsqrt(jnp.mean(hidden * hidden, axis=1, keepdims=True) + norm_eps)
    normed = (hidden * scale * gain).astype(BF)
    normed_ref[0] = normed
    cot = cot_ref[0]
    out = hidden
    grad_mid = jnp.zeros((rows, width), F32)
    for j in range(active_ref.shape[0]):
        if wb.shape[0] == 1:
            down = wb[0, 0, j]
        else:
            owners = wb.shape[0] // active_ref.shape[0]
            down = wb[j * owners : (j + 1) * owners].reshape(width, width)
        up = wa[1 + j].reshape(width, width)
        u = dot(normed, up, ((1,), (0,)))
        ga = dot(cot, down, ((1,), (1,)))
        square = u * u
        t = jnp.tanh(u * (gelu_slope + gelu_slope * gelu_cubic * square))
        plus = 0.5 + 0.5 * t
        active = (u * plus).astype(BF)
        slope = plus + (0.5 * u) * (1.0 - t * t) * (
            gelu_slope + 3.0 * gelu_slope * gelu_cubic * square
        )
        up_grad = (ga * slope).astype(BF)
        active_ref[j, 0] = active
        up_grad_ref[j, 0] = up_grad
        out = out + dot(active, down, ((1,), (0,)))
        grad_mid = grad_mid + dot(up_grad, up, ((1,), (1,)))
    output_ref[0] = out.astype(BF)
    gain_grad_ref[...] += jnp.sum(grad_mid * hidden * scale, axis=0, keepdims=True)
    weighted = grad_mid * gain
    inner = jnp.mean(weighted * hidden, axis=1, keepdims=True)
    grad_hidden = cot.astype(F32) + scale * weighted - hidden * (scale * scale * scale * inner)
    grad_hidden_ref[0] = grad_hidden
    hidden_bf = grad_hidden.astype(BF)
    hidden_bf_ref[0] = hidden_bf
    grad_mixed = dot(hidden_bf, w_out, ((1,), (1,))).astype(BF)
    place = pl.ds(pl.multiple_of(step * rows, rows), rows)
    cuts = []
    for ref in group_refs:
        first = cuts[-1].stop if cuts else 0
        cuts.append(slice(first, first + ref.shape[2]))
        ref[0, place, :] = grad_mixed[:, cuts[-1]]
    product[...] += grad_mixed.astype(F32) * mixed.astype(F32)

    @pl.when(step == pl.num_programs(0) - 1)
    def _():
        for ref, cut in zip(group_refs, cuts):
            lanes = cut.stop - cut.start
            head = lax.broadcasted_iota(jnp.int32, (8, lanes), 0)
            lane = lax.broadcasted_iota(jnp.int32, (8, lanes), 1)
            terms = lax.dot_general(
                jnp.where((lane >> 6) == head, 1.0, 0.0),
                product[:, cut],
                (((1,), (1,)), ((), ())),
                precision=lax.Precision.HIGHEST,
                preferred_element_type=F32,
            )
            ref[0, ref.shape[1] - 16 :, :rows] = two_parts(terms)


def two_parts(x):
    high = x.astype(BF).astype(F32)
    return jnp.concatenate([high, x - high], axis=0).astype(BF)


def one_part(x):
    count = x.shape[0] // 2
    x = x.astype(F32)
    return x[:count] + x[count:]


def feed_forward(core, own, got, tokens, cot, gain, parts, group_heads):
    seqs, rows, width = tokens.shape
    n_seq, units, chips, part_rows, _ = own.shape
    count = (units - 1) // 2
    act = pl.BlockSpec((1, rows, width), lambda s, _: (s, 0, 0))
    wide = pl.BlockSpec((count, 1, rows, width), lambda s, _: (0, s, 0, 0))
    payloads = [(1, seqs * rows + 16, 64 * heads) for heads in group_heads]
    anywhere = pl.BlockSpec(memory_space=pl.ANY)
    gain_spec = pl.BlockSpec((1, width), lambda s, _: (0, 0))
    act_bf = jax.ShapeDtypeStruct(tokens.shape, BF)
    wide_bf = jax.ShapeDtypeStruct((count, *tokens.shape), BF)
    tokens_all = seqs * rows
    return pl.pallas_call(
        functools.partial(ffn_kernel, len(parts)),
        grid_spec=pltpu.PrefetchScalarGridSpec(
            num_scalar_prefetch=1,
            grid=(seqs,),
            in_specs=[anywhere] * 2 + [act, act, gain_spec] + [act] * len(parts),
            out_specs=[act, act, act, wide, wide, act, act]
            + [pl.BlockSpec(payload, lambda s, _: (0, 0, 0)) for payload in payloads]
            + [gain_spec],
            scratch_shapes=[
                pltpu.VMEM((1 + count, n_seq, chips, part_rows, width), BF),
                pltpu.VMEM((n_seq, chips, count, part_rows, width), BF),
                pltpu.VMEM((rows, width), F32),
                pltpu.SemaphoreType.DMA((2, units)),
            ],
        ),
        out_shape=[act_bf] * 3
        + [wide_bf] * 2
        + [jax.ShapeDtypeStruct(tokens.shape, F32), act_bf]
        + [jax.ShapeDtypeStruct(payload, BF) for payload in payloads]
        + [jax.ShapeDtypeStruct((1, width), F32)],
        compiler_params=params(),
        cost_estimate=cost(SHORT),
        name="feed_forward",
    )(core, own, got, tokens, cot, gain, *parts)


def write_halves(core, grad, keep_ref, send_ref):
    half = keep_ref.shape[-1]
    for c in range(2):

        @pl.when(core == c)
        def _(c=c):
            keep_ref[0] = grad[:, c * half : c * half + half]
            send_ref[0] = grad[:, half - c * half : 2 * half - c * half]


def grads_kernel(first, core_ref, *refs):
    keep_ref, send_ref = refs[-2:]
    ins = refs[: 4 if first else 2]

    def write(left, right):
        grad = dot(
            left[...].reshape(left.shape[-2:]), right[...].reshape(right.shape[-2:]), ((0,), (0,))
        )
        write_halves(core_ref[0], grad.astype(BF), keep_ref, send_ref)

    if first:
        pl.when(pl.program_id(0) == 0)(lambda: write(ins[0], ins[1]))
        pl.when(pl.program_id(0) > 0)(lambda: write(ins[2], ins[3]))
    else:
        write(*ins)


def weight_grads(core, name, one, many, into=()):
    first = 1 if one else 0
    units = first + max(a.shape[0] for a in many if a.ndim == 3)
    rows, width = many[0].shape[-2:]

    def spec(a):
        if a.ndim == 2:
            return pl.BlockSpec((rows, width), lambda u, _: (0, 0))
        return pl.BlockSpec((1, rows, width), lambda u, _: (jnp.maximum(u - first, 0), 0, 0))

    ins = [*one, *many]
    out = pl.BlockSpec((1, width, width // 2), lambda u, _: (u, 0, 0))
    total = into[0].shape[0] if into else units
    return pl.pallas_call(
        functools.partial(grads_kernel, first),
        grid_spec=pltpu.PrefetchScalarGridSpec(
            num_scalar_prefetch=1,
            grid=(units,),
            in_specs=[spec(a) for a in ins] + [pl.BlockSpec(memory_space=pl.ANY)] * len(into),
            out_specs=[out, out],
        ),
        out_shape=[jax.ShapeDtypeStruct((total, width, width // 2), BF)] * 2,
        input_output_aliases={1 + len(ins) + i: i for i in range(len(into))},
        compiler_params=params(),
        cost_estimate=cost(SHORT),
        name=name,
    )(core, *ins, *into)


def pair_of(step, place_ref, split):
    return (1 - step) ^ place_ref[1] if split else step


def backward_kernel(blocks, split, place_ref, attention_ref, values_ref, *refs):
    grads, terms, refs = refs[:blocks], refs[blocks : 2 * blocks], refs[2 * blocks :]
    *outs, grad_values_ref, acc_ref, all_ref = refs
    step = pl.program_id(0)
    pair = pair_of(step, place_ref, split)
    _, length, width = attention_ref.shape
    seqs = values_ref.shape[0]
    me = place_ref[0]
    values = split_heads(jnp.concatenate([values_ref[s] for s in range(seqs)], axis=1))
    lane = lax.broadcasted_iota(jnp.int32, (width, 8), 1)

    for r in range(blocks):
        q = me ^ r

        @pl.when(q >= me)
        def _(r=r, q=q):
            rows = pl.ds(pl.multiple_of(q * width, width), width)
            grad = jnp.concatenate(
                [grads[r][0, s * width : (s + 1) * width, :] for s in range(seqs)], axis=1
            )
            scores = dot(grad, values, ((1,), (1,)))
            table = one_part(terms[r][0][:, :width]).T
            for h in range(2):
                term = jnp.sum(jnp.where(lane == pair * 2 + h, table, 0.0), axis=1, keepdims=True)
                a = attention_ref[h, rows, :].astype(F32)
                grad_a = (a * (scores[:, h * width : (h + 1) * width] - term)).astype(BF)
                all_ref[h, r] = grad_a
            part = dot(
                jnp.concatenate([attention_ref[0, rows, :], attention_ref[1, rows, :]], axis=0),
                split_heads(grad),
                ((0,), (0,)),
            )
            if r == 0:
                acc_ref[...] = part
            else:
                acc_ref[...] += part

        if r:

            @pl.when(q < me)
            def _(r=r):
                for h in range(2):
                    all_ref[h, r] = jnp.zeros((width, width), BF)

    if split:
        for i, out in enumerate(outs):

            @pl.when(step == i)
            def _(out=out):
                out[...] = all_ref[...]

    else:
        outs[0][...] = all_ref[...]

    total = acc_ref[...].astype(BF)
    for s in range(seqs):
        grad_values_ref[s] = total[:, s * 128 : s * 128 + 128]


def mix_backward(place, attention, values, grads, first, split):
    blocks = len(grads)
    _, length, width = attention.shape
    seqs = values.shape[0]
    lanes = grads[0].shape[2]
    pairs = lanes // 128
    before = first // 2

    def pair(m, at):
        return pair_of(m, at, split)

    part = pl.BlockSpec((1, seqs * width, 128), lambda m, at: (0, 0, pair(m, at)))
    terms = pl.BlockSpec((1, 16, lanes), lambda m, _: (0, seqs * width // 16, 0))
    out = pl.BlockSpec((2, blocks, width, width), lambda m, _: (0 if split else m, 0, 0, 0))
    outs = 2 if split else 1
    rows = 2 if split else 2 * pairs
    return pl.pallas_call(
        functools.partial(backward_kernel, blocks, split),
        grid_spec=pltpu.PrefetchScalarGridSpec(
            num_scalar_prefetch=1,
            grid=(pairs,),
            in_specs=[
                pl.BlockSpec((2, length, width), lambda m, at: (pair(m, at) + before, 0, 0)),
                pl.BlockSpec((seqs, width, 128), lambda m, at: (0, 0, pair(m, at) + before)),
            ]
            + [part] * blocks
            + [terms] * blocks,
            out_specs=[out] * outs
            + [pl.BlockSpec((seqs, width, 128), lambda m, at: (0, 0, pair(m, at)))],
            scratch_shapes=[
                pltpu.VMEM((width, seqs * 128), F32),
                pltpu.VMEM((2, blocks, width, width), BF),
            ],
        ),
        out_shape=[jax.ShapeDtypeStruct((rows, blocks, width, width), BF)] * outs
        + [jax.ShapeDtypeStruct((seqs, width, lanes), BF)],
        compiler_params=params(),
        cost_estimate=cost((MIX0, MIX1, MIX2)[first // 4 % 3]),
        name="mix_backward",
    )(place, attention, values, *grads, *grads)


def logits_adam_kernel(place_ref, weight_ref, first_ref, second_ref, *refs):
    grads, outs = refs[:4], refs[-3:]
    q = pl.program_id(1)
    me = place_ref[0]

    def update(h, gradient):
        weight = weight_ref[h]
        first = beta_first * first_ref[h]
        second = beta_second * second_ref[h]
        if gradient is not None:
            first = first + (1.0 - beta_first) * gradient
            second = second + ((1.0 - beta_second) * gradient) * gradient
        root = second * lax.rsqrt(second)
        bottom = root * math.sqrt(1.0 / (1.0 - beta_second**STEP)) + adam_eps
        step = first * (1.5 / (1.0 - beta_first**STEP)) / bottom
        outs[0][h] = weight * (1.0 - 1.5 * weight_decay) - step
        outs[1][h] = first
        outs[2][h] = second

    @pl.when(q >= me)
    def _():
        for h in range(4):
            update(h, grads[h][0, 0, 0].astype(F32))

    @pl.when(q < me)
    def _():
        for h in range(4):
            update(h, None)


def logits_adam(place, logits, first, second, pieces, group, start, before):
    heads, length, width = logits.shape
    blocks = length // width
    n_seq, groups, rows, _ = pieces.shape
    per = rows // width
    part = pl.BlockSpec((4, width, width), lambda k, q, _: (k + start // 4, q, 0))

    def owner(h, r):
        out = (h >> 1) + 2 * (h & 1)
        left, bit = blocks // 2, 4
        while left >= per:
            out = out + bit * ((r // left) % 2)
            left, bit = left // 2, bit * 2
        return out

    def grad(h):
        def index(k, q, at):
            r = jnp.where(q >= at[0], q ^ at[0], 0)
            return (owner(h, r), k + group, r % per, 0, 0)

        return pl.BlockSpec((1, 1, 1, width, width), index)

    ins = [logits, first, second] + [pieces.reshape(n_seq, groups, per, width, width)] * 4
    specs = [part] * 3 + [grad(h) for h in range(4)]
    aliases = {}
    if before is not None:
        aliases = {1 + len(ins) + i: i for i in range(3)}
        ins += list(before)
        specs += [pl.BlockSpec(memory_space=pl.ANY)] * 3
    return pl.pallas_call(
        logits_adam_kernel,
        grid_spec=pltpu.PrefetchScalarGridSpec(
            num_scalar_prefetch=1,
            grid=(1, blocks),
            in_specs=specs,
            out_specs=[part] * 3,
        ),
        out_shape=[jax.ShapeDtypeStruct(logits.shape, F32)] * 3,
        input_output_aliases=aliases,
        compiler_params=params(),
        cost_estimate=cost(UPDATE),
        name="logits_adam",
    )(place, *ins)


def input_kernel(groups, core_ref, *refs):
    grads, refs = refs[:groups], refs[groups:]
    (normed_ref, tokens_ref, value_ref, hidden_ref, gain_ref), refs = refs[:5], refs[5:]
    input_grad_ref, gain_grad_ref, keep_ref, send_ref, acc_ref = refs
    step = pl.program_id(0)
    grad = jnp.concatenate([ref[0] for ref in grads], axis=1)
    product = dot(normed_ref[0], grad, ((0,), (0,)))
    gain = gain_ref[...]
    tokens = tokens_ref[0].astype(F32)
    scale = lax.rsqrt(jnp.mean(tokens * tokens, axis=1, keepdims=True) + norm_eps)
    grad_in = dot(grad, value_ref[...], ((1,), (1,)))
    gain_part = jnp.sum(grad_in * tokens * scale, axis=0, keepdims=True)
    weighted = grad_in * gain
    inner = jnp.mean(weighted * tokens, axis=1, keepdims=True)
    total = hidden_ref[0] + scale * weighted - tokens * (scale * scale * scale * inner)
    input_grad_ref[0] = total.astype(BF)

    @pl.when(step == 0)
    def _():
        acc_ref[...] = product
        gain_grad_ref[...] = gain_part

    @pl.when(step > 0)
    def _():
        acc_ref[...] += product
        gain_grad_ref[...] += gain_part

    @pl.when(step == pl.num_programs(0) - 1)
    def _():
        write_halves(core_ref[0], acc_ref[...].astype(BF), keep_ref, send_ref)


def input_backward(core, grads, normed, tokens, value, hidden, gain):
    seqs, rows, width = tokens.shape
    act = pl.BlockSpec((1, rows, width), lambda s, _: (s, 0, 0))
    gain_spec = pl.BlockSpec((1, width), lambda s, _: (0, 0))
    half = pl.BlockSpec((1, width, width // 2), lambda s, _: (0, 0, 0))
    return pl.pallas_call(
        functools.partial(input_kernel, len(grads)),
        grid_spec=pltpu.PrefetchScalarGridSpec(
            num_scalar_prefetch=1,
            grid=(seqs,),
            in_specs=[
                pl.BlockSpec((1, rows, grad.shape[2]), lambda s, _: (s, 0, 0)) for grad in grads
            ]
            + [act, act, pl.BlockSpec((width, width), lambda s, _: (0, 0)), act, gain_spec],
            out_specs=[act, gain_spec, half, half],
            scratch_shapes=[pltpu.VMEM((width, width), F32)],
        ),
        out_shape=[
            jax.ShapeDtypeStruct(tokens.shape, BF),
            jax.ShapeDtypeStruct((1, width), F32),
            jax.ShapeDtypeStruct((1, width, width // 2), BF),
            jax.ShapeDtypeStruct((1, width, width // 2), BF),
        ],
        compiler_params=params(),
        cost_estimate=cost(SHORT),
        name="input_backward",
    )(core, *grads, normed, tokens, value, hidden, gain)


def bundle_kernel(keep_a, got_a, keep_b, got_b, out_ref):
    a = keep_a[...].astype(F32) + got_a[...].astype(F32)
    b = keep_b[...].astype(F32) + got_b[...].astype(F32)
    units = a.shape[0]
    out_ref[0, :units] = a[:, 0].astype(BF)
    out_ref[0, units:] = b[0].astype(BF)


def bundle(keep_a, got_a, keep_b, got_b):
    units, owners, rows, columns = keep_a.shape
    units_b = keep_b.shape[1]
    spec_a = pl.BlockSpec((units, 1, rows, columns), lambda g: (0, g, 0, 0))
    spec_b = pl.BlockSpec((1, units_b, rows, columns), lambda g: (g, 0, 0, 0))
    return pl.pallas_call(
        bundle_kernel,
        grid=(owners,),
        in_specs=[spec_a, spec_a, spec_b, spec_b],
        out_specs=pl.BlockSpec((1, units + units_b, rows, columns), lambda g: (g, 0, 0, 0)),
        out_shape=jax.ShapeDtypeStruct((owners, units + units_b, rows, columns), BF),
        compiler_params=params(),
        cost_estimate=cost(SHORT),
        name="bundle",
    )(keep_a, got_a, keep_b, got_b)


def merge_kernel(bit_ref, keep, got, value_keep, value_got, send_ref, keep_ref):
    value = (value_keep[:, 0].astype(F32) + value_got[:, 0].astype(F32)).astype(BF)
    others = (keep[:, 0].astype(F32) + got[:, 0].astype(F32)).astype(BF)
    for i, out in enumerate((send_ref, keep_ref)):

        @pl.when(pl.program_id(0) == i)
        def _(out=out):
            out[:, : others.shape[1]] = others
            out[:, others.shape[1] :] = value


def merge_halves(terms, step):
    n, _, units, rows, columns = terms[0].shape
    total = units + terms[2].shape[2]

    def spec(count):
        return pl.BlockSpec(
            (size, 1, count, rows, columns), lambda i, g, bit: (g, bit[0] ^ (1 - i), 0, 0, 0)
        )

    size = max(1, n // 4)
    last = n // size - 1
    block = (size, total, rows, columns)
    return pl.pallas_call(
        merge_kernel,
        grid_spec=pltpu.PrefetchScalarGridSpec(
            num_scalar_prefetch=1,
            grid=(2, n // size),
            in_specs=[spec(t.shape[2]) for t in terms],
            out_specs=[
                pl.BlockSpec(block, lambda i, g, _: (g * (1 - i) + last * i, 0, 0, 0)),
                pl.BlockSpec(block, lambda i, g, _: (g * i, 0, 0, 0)),
            ],
        ),
        out_shape=[jax.ShapeDtypeStruct((n, total, rows, columns), BF)] * 2,
        compiler_params=params(),
        cost_estimate=cost(SHORT),
        name="merge_halves",
    )(bit_array(step), *terms)


def whole_tiles(pieces, units):
    n_seq, _, chips, rows, half = pieces.shape
    a = pieces[:, : 1 + units].transpose(1, 0, 2, 3, 4)
    b = pieces[:, 1 + units :].transpose(0, 2, 1, 3, 4).reshape(units, -1, *a.shape[-1:])
    full = jnp.concatenate([a.reshape(1 + units, -1, half), b], axis=0)
    return full.reshape(1, 1 + 2 * units, 1, -1, half)


def body(
    tokens,
    cotangent,
    gains,
    gain_first,
    gain_second,
    mix_logits,
    logit_first,
    logit_second,
    w_value,
    value_first,
    value_second,
    w_out,
    out_first,
    out_second,
    w_up,
    up_first,
    up_second,
    w_down,
    down_first,
    down_second,
):
    head_count, length, width_pos = mix_logits.shape
    positions, seq_count, width = tokens.shape
    hidden_width = w_up.shape[1]
    token_rows = positions * seq_count
    units = hidden_width // width
    half = width // 2
    n_pos, n_seq = lax.axis_size("pos"), lax.axis_size("seq")
    pos = lax.axis_index("pos")
    pos_array = pos.astype(jnp.int32).reshape(1)
    place = jnp.stack([pos, bit_value("seq", 0)]).astype(jnp.int32)
    core = pos & 1
    core_array = core.astype(jnp.int32).reshape(1)
    chip = pos >> 1
    chips = n_pos // 2
    seq_low, pos_low = ("seq", 0), ("pos", 0)
    far = chip_bits("seq")
    across = chip_bits("pos")


    def own_piece(weight):
        rows, columns = weight.shape
        part = lax.dynamic_slice_in_dim(weight, chip * (rows // chips), rows // chips, 0)
        part = part.reshape(rows // chips, columns // width, 2, half)
        return lax.dynamic_index_in_dim(part, core, 2, keepdims=False).astype(BF)

    def both_halves(own, other):
        return jnp.where(
            core == 1,
            jnp.concatenate([other, own], axis=-1),
            jnp.concatenate([own, other], axis=-1),
        )

    away = far + across + [seq_low]
    value = Gather(own_piece(w_value)[:, 0], away, 0)
    part_rows = w_up.shape[0] // chips

    def other_pieces(out, up, down):
        a = jnp.concatenate([own_piece(out), own_piece(up)], axis=1).transpose(1, 0, 2)
        return jnp.concatenate([a, own_piece(down).reshape(units, part_rows, half)], axis=0)

    others = Gather(behind(other_pieces(w_out, w_up, w_down), (value.out,), LONG), across, 1)
    totals = row_totals(pos_array, mix_logits, n_pos, (value.out, others.out))
    totals_got = swap(totals, "pos", 1)
    for _ in across:
        others.next((totals,), FRONT)
    others = others.result()
    last = others
    others = lax.all_gather(others, "seq", axis=0, tiled=False)

    tokens_rows, cot_rows = tokens.transpose(1, 0, 2), cotangent.transpose(1, 0, 2)
    tokens_wide = tokens_rows.reshape(token_rows, width).astype(F32)
    in_scale = lax.rsqrt(jnp.mean(tokens_wide * tokens_wide, axis=-1, keepdims=True) + norm_eps)
    normed_in = (tokens_wide * in_scale * gains[0]).astype(BF)
    for _ in far[1:]:
        value.next((last, totals), 1)
    for _, bit in across:
        totals = behind(totals_got, (value.out,), 1) + totals
        totals_got = swap(totals, "pos", 1 << bit)
    value.next((totals,), 1)
    for _ in across:
        value.next((normed_in,), 1)
    scale = 1.0 / (behind(totals_got, (value.out,), 1) + totals)
    attention = attention_of(pos_array, mix_logits, scale, n_pos)
    value.next((attention,), 1)
    value_half = value.result()
    value_other = swap(value_half, "pos", 1)
    value_full = both_halves(value_half, value_other)
    values = jnp.dot(normed_in, value_full, preferred_element_type=F32).astype(BF)
    values = values.reshape(seq_count, positions, width)
    parts, sent = send_to_queries(mix_forward(pos_array, attention, values, n_pos))
    others = behind(others, (sent,), 1).reshape(n_seq, 1 + 2 * units, chips, part_rows, half)
    if part_rows % 16:
        others = whole_tiles(others, units)
    others_got = swap(others, "pos", 1)
    parts[-1] = behind(parts[-1], (others,), LONG)
    (
        output,
        mixed,
        normed_mid,
        active,
        up_grad,
        grad_hidden,
        hidden_bf,
        *payloads,
        gain_mid,
    ) = feed_forward(
        core_array,
        others,
        others_got,
        tokens_rows,
        cot_rows,
        gains[1:2],
        parts,
        GROUP_HEADS,
    )

    def placed(x):
        return x.transpose(1, 0, 2)

    def rows_of(x):
        return x.reshape(*x.shape[:-3], token_rows, width)

    near = [gather_queries(part, [0])[1] for part in payloads]
    arrived = [gather_queries(part, [b for _, b in reversed(across)]) for part in payloads]
    keep_b, send_b = weight_grads(
        core_array, "grads_down", (), (rows_of(active), rows_of(cot_rows))
    )
    last = keep_b
    chains, grad_values = [], []
    keep_a = send_a = got_a = got_b = keep_w = got_w = value_terms = None
    chain = chain_a = chain_b = merged = owned = gain_total = input_grad = logits_out = None
    gain_steps = [pos_low] + across + far + [seq_low]

    def mixing_step():
        nonlocal last
        k = len(chains)
        for r in arrived[k]:
            if r:
                arrived[k][r] = behind(arrived[k][r], (last,), SHORT)
        blocks = gather_queries(None, [0], {**arrived[k], 1: near[k]})
        send, keep, grad_values_k = mix_backward(
            place,
            attention,
            values,
            [blocks[r] for r in range(n_pos)],
            sum(GROUP_HEADS[:k]),
            True,
        )
        grad_values.append(grad_values_k)
        chains.append(HalvesOut(send, keep, [seq_low] + far))
        last = send

    def grads_step():
        nonlocal keep_a, send_a, last
        keep_a, send_a = weight_grads(
            core_array,
            "grads_others",
            (rows_of(mixed), rows_of(hidden_bf)),
            (rows_of(normed_mid), behind(rows_of(up_grad), (last,), SHORT)),
        )
        last = keep_a

    def core_step():
        nonlocal got_a, got_b, last
        last = behind(send_a, (last,), SHORT)
        got_a, got_b = swap(last, "pos", 1), swap(send_b, "pos", 1)

    def input_step():
        nonlocal input_grad, gain_total, value_terms, last
        input_grad, gain_in, keep, send = input_backward(
            core_array,
            [behind(grad_values[0], (last,), SHORT), *grad_values[1:]],
            normed_in.reshape(tokens_rows.shape),
            tokens_rows,
            value_full,
            grad_hidden,
            gains[0:1],
        )
        gain_total = jnp.concatenate([gain_in, gain_mid], axis=0)
        value_terms = [keep, swap(send, "pos", 1)]
        last = keep

    def value_step():
        nonlocal value_terms, last
        value_terms[1] = behind(value_terms[1], (last,))
        for step in across:
            views = [t.reshape(-1, 2, part_rows, half) for t in value_terms]
            last, keep = halves_sum(views, step)
            value_terms = [keep, swap(last, "pos", 1 << step[1])]

    def bundle_step():
        nonlocal chain_a, chain_b, last
        dims = list(reversed(far)) + [seq_low] + list(reversed(across))
        chain_a = RowSum(keep_a, got_a, 1 + units, across + [seq_low], dims)
        chain_b = RowSum(keep_b.reshape(-1, half), got_b.reshape(-1, half), 1, across, dims)
        for _ in across:
            last = chain_a.next((last,))
        for _ in across:
            last = chain_b.next((last,))

    def projections_step():
        nonlocal chain, merged, owned, last
        owners = n_seq // 2
        if chain_a.steps:
            last = chain_a.next((last,))
        elif merged is None:
            shape = (owners, 2, -1, part_rows, half)
            terms = [
                x.reshape(shape)
                for x in (chain_b.keep, behind(chain_b.got, (last,)), *value_terms)
            ]
            last, keep = merge_halves(terms, seq_low)
            merged = [keep, swap(last, "seq", 1)]
        elif chain is None:
            a = [t.reshape(1 + units, owners, part_rows, half) for t in (chain_a.keep, chain_a.got)]
            b = [t.reshape(owners, 1 + units, part_rows, half) for t in merged]
            b[1] = behind(b[1], (last,))
            total = bundle(*a, *b)
            steps = list(far)
            step = steps.pop(0)
            left = [d for d in reversed(far)]
            view = total.reshape(1 << left.index(step), 2, -1, half)
            last, keep = halves_sum([view], step)
            left.remove(step)
            chain = RowSum(keep.reshape(-1, half), None, 1, steps, left)
            chain.got = swap(last, "seq", 1 << step[1]).reshape(-1, half)
        elif chain.steps:
            last = chain.next((last, placed(output), placed(input_grad)))
        elif owned is None:
            keep, got = (t.reshape(-1, half) for t in (chain.keep, chain.got))
            last = sum_of(keep, behind(got, (last,)))
            owned = Gather(last.reshape(2 + 2 * units, part_rows, half), list(reversed(across)), 1)
        elif owned.steps:
            owned.next((last,))
            last = owned.out

    def gain_step():
        nonlocal gain_total, last
        if gain_steps:
            axis, bit = gain_steps.pop(0)
            last = gain_total = behind(gain_total, (last,))
            gain_total = gain_total + swap(gain_total, axis, 1 << bit)

    def sum_step(k):
        nonlocal last
        if chains[k].steps:
            chains[k].next((last,))
            last = chains[k].send

    def gather_step(groups):
        nonlocal last
        for k in groups:
            while chains[k].steps:
                sum_step(k)
        pairs = [(chains[k].keep, chains[k].got) for k in groups]
        pairs[0] = (pairs[0][0], behind(pairs[0][1], (last,)))
        last = pieces_of(pairs)
        gathered[groups[0]] = lax.all_gather(last, "seq", axis=0, tiled=False)

    def update(k):
        nonlocal logits_out, last
        groups = next(g for g in parts_of if k in g)
        if groups[0] not in gathered:
            gather_step(groups)
        if k == groups[0]:
            gathered[groups[0]] = behind(gathered[groups[0]], (last,))
        logits_out = logits_adam(
            place,
            mix_logits,
            logit_first,
            logit_second,
            gathered[groups[0]],
            k - groups[0],
            sum(GROUP_HEADS[:k]),
            logits_out,
        )
        last = logits_out[0]

    steps = {
        "m": mixing_step,
        "u": grads_step,
        "c": core_step,
        "b": bundle_step,
        "w": projections_step,
        "i": input_step,
        "v": value_step,
        "g": gain_step,
    }
    for k in range(len(GROUP_HEADS)):
        steps[str(k)] = functools.partial(sum_step, k)
    gathered = {}
    parts_of = [0], list(range(1, len(GROUP_HEADS)))
    for name, k in zip("pq", parts_of):
        steps[name] = functools.partial(gather_step, k)
    for k in range(len(GROUP_HEADS)):
        steps[str(k + 3)] = functools.partial(update, k)
    for name in PLAN:
        steps[name]()
    while gain_steps:
        gain_step()
    while owned is None or owned.steps:
        projections_step()
    logits_new, logit_first_new, logit_second_new = logits_out
    owned = owned.result()
    owned = both_halves(owned, swap(owned, "pos", 1)).astype(F32)
    grad_out, grad_value = owned[0], owned[1 + 2 * units]
    grad_up = jnp.concatenate([owned[1 + j] for j in range(units)], axis=1)
    grad_down = owned[1 + units : 1 + 2 * units].reshape(units, chips, part_rows, width)
    grad_down = grad_down.transpose(1, 0, 2, 3).reshape(-1, width)
    gains_new, gain_first_new, gain_second_new = adam_update(
        gains, gain_first, gain_second, gain_total, 0.8, 0.0
    )
    value_new, value_first_new, value_second_new = adam_update(
        w_value, value_first, value_second, grad_value, 1.0 / math.sqrt(width), weight_decay
    )
    out_new, out_first_new, out_second_new = adam_update(
        w_out,
        out_first,
        out_second,
        grad_out,
        1.0 / math.sqrt(width * 16 // length),
        weight_decay,
    )
    up_new, up_first_new, up_second_new = adam_update(
        w_up, up_first, up_second, grad_up, 1.0 / math.sqrt(width), weight_decay
    )
    down_new, down_first_new, down_second_new = adam_update(
        w_down, down_first, down_second, grad_down, 1.0 / math.sqrt(hidden_width), weight_decay
    )
    return (
        placed(output),
        placed(input_grad),
        gains_new,
        gain_first_new,
        gain_second_new,
        logits_new,
        logit_first_new,
        logit_second_new,
        value_new,
        value_first_new,
        value_second_new,
        out_new,
        out_first_new,
        out_second_new,
        up_new,
        up_first_new,
        up_second_new,
        down_new,
        down_first_new,
        down_second_new,
    )


def solution(mesh):
    activations = P("pos", "seq", None)
    logits = P(None, None, "pos")
    rows = P("seq", None)
    placed = (activations,) * 2 + (P(),) * 3 + (logits,) * 3 + (rows,) * 12
    return jax.shard_map(
        body, mesh=mesh, in_specs=placed, out_specs=placed, check_vma=False
    )
```
